32 devices in a mesh: cell: 8 (over z, x), spot: 4 (over y, core).
Axes of the slice: x: 2, y: 2, z: 4, core: 2. Of those that a mesh axis runs over, the one named last changes fastest.
Arguments:
- logits: float32 [32768, 2048], P('cell', 'spot'), may hold values from -8 to 8
- expression: bfloat16 [32768, 2048], P('cell'), may hold values from 0.099609375 to 10
- target: float32 [2048, 2048], P('cell', 'spot'), may hold values from 0.1 to 10
- keep_mask: int32 [32768], P('cell'), may hold values from 0 to 1, as said below
- slide_ids: int32 [2048], P('spot'), may hold values from 0 to 7, as said below
- slide_counts: int32 [8], replicated, may hold values from 64 to 768, as said below
Outputs:
- mapping_loss: float32 [], replicated
- predicted: float32 [2048, 2048], P('cell', 'spot')
- grad_logits: float32 [32768, 2048], P('cell', 'spot')
- grad_expression: float32 [32768, 2048], P('cell', 'spot')
The draws below stay inside these ranges and needn't reach their ends.
Inputs may be any that keep to these rules, and one draw needn't show every extreme that they name: `keep_mask`: the first cell of every aligned block of 4096 cells is kept. `slide_ids`: every slide has at least 64 spots and at most 768. slide_counts[k] is the number of spots whose slide id is k.
All inputs are finite; a program needn't handle non-finite values.
Results may differ from the reference program's by a relative error of at most 0.0043.
Values may be sent and summed in bfloat16 or wider, within the bound.
No kernel may reach another device: no remote copies, remote signals or barrier semaphores. Data moves between devices by JAX's collectives and lax.ppermute only.
A program may use at most 192 MiB of HBM per device.

```python
import math
import jax
import jax.numpy as jnp
from jax import lax

NG = 2048
CELL_DEV = 4096
NSLIDE = 8
NC = 32768
NS = 2048


def slide_layout(key):
    random_ids = jax.random.randint(jax.random.fold_in(key, 11), (NS,), 0, NSLIDE - 2)
    shuffle = jax.random.permutation(jax.random.fold_in(key, 12), NS)
    big_slide = jax.random.randint(jax.random.fold_in(key, 13), (), 0, NSLIDE).astype(jnp.int32)
    floor_count = NS // (4 * NSLIDE)
    most_count = 3 * NS // 8
    position = jnp.arange(NS, dtype=jnp.int32)
    cyclic = position % NSLIDE
    big_start = floor_count * NSLIDE
    rest_start = big_start + most_count - floor_count
    rest_total = NS - rest_start
    offset = position - rest_start
    cyclic_other = offset % (NSLIDE - 2)
    pick_other = jnp.where(offset < rest_total // 2, cyclic_other, random_ids)
    other_slide = (big_slide + 1 + pick_other) % NSLIDE
    assigned = jnp.where(position < big_start, cyclic, jnp.where(position < rest_start, big_slide, other_slide))
    slide_of = jnp.zeros((NS,), jnp.int32).at[shuffle].set(assigned.astype(jnp.int32))
    tally = jnp.sum((slide_of[:, None] == jnp.arange(NSLIDE, dtype=jnp.int32)[None, :]).astype(jnp.int32), axis=0)
    return (slide_of, tally)


def draw_slide_ids(key, part):
    slide_of, tally = slide_layout(key)
    return slide_of


def draw_slide_counts(key, part):
    slide_of, tally = slide_layout(key)
    return tally


def draw_keep_mask(key, part):
    key = jax.random.fold_in(key, 3)
    block_count = NC // CELL_DEV
    cell_index = jnp.arange(NC, dtype=jnp.int32)
    block_index = cell_index // CELL_DEV
    threshold = 30 + 65 * block_index // max(block_count - 1, 1)
    dice_roll = jax.random.randint(key, (NC,), 0, 100)
    kept = (dice_roll < threshold) | (cell_index % CELL_DEV == 0)
    return kept.astype(jnp.int32)


def block_levels(rng, extent, shards, low, top_value):
    loudness = 1.0
    for dim, shards_of in shards:
        draws = jax.random.uniform(jax.random.fold_in(jax.random.fold_in(rng, 6), dim), (shards_of,), jnp.float32, low / len(shards), top_value / len(shards))
        loudness = loudness * jnp.repeat(jnp.exp(draws), extent[dim] // shards_of).reshape((-1,) + (1,) * (len(extent) - 1 - dim))
    return loudness


def scatter_about(stream_key, extent, scale, most, shards=(), kind=jnp.bfloat16):
    values = scale * jax.random.normal(stream_key, extent, jnp.float32)
    if shards:
        values = values * block_levels(stream_key, extent, shards, -0.22, 0.18)
    return jnp.clip(values, -most, most).astype(kind)


def setup_inputs(seed: int = 0) -> dict:
    splits = jax.random.split(jax.random.key(seed), 7)
    return {
        "logits": scatter_about(splits[0], (NC, NS), 2.0, 8.0, ((0, 8), (1, 4)), jnp.float32),
        "expression": jnp.clip(jnp.exp(math.log(10.0) - 4.609084 * jax.random.uniform(splits[1], (NC, NG), jnp.float32) ** block_levels(splits[1], (NC, NG), ((0, 8),), -0.2, 0.2)), 0.099609375, 10.0).astype(jnp.bfloat16),
        "target": jnp.clip(jnp.exp(math.log(10.0) - 4.6051702 * jax.random.uniform(splits[2], (NG, NS), jnp.float32) ** block_levels(splits[2], (NG, NS), ((0, 8), (1, 4)), -0.2, 0.2)), 0.1, 10.0),
        "keep_mask": draw_keep_mask(jax.random.fold_in(splits[6], 71), 0),
        "slide_ids": draw_slide_ids(jax.random.fold_in(splits[6], 71), 0),
        "slide_counts": draw_slide_counts(jax.random.fold_in(splits[6], 71), 0),
    }


@jax.custom_vjp
def low(v):
    return lax.optimization_barrier(v.astype(jnp.bfloat16)).astype(jnp.float32)

@jax.custom_vjp
def low_back(v):
    return v

def low_keep(v):
    return (low(v), None)

def low_pass(kept, grad):
    return (grad,)

def back_keep(v):
    return (v, None)

def back_low(kept, grad):
    return (low(grad),)
low.defvjp(low_keep, low_pass)
low_back.defvjp(back_keep, back_low)
density_weight = 32.0
expression_scale = 64.0
norm_eps = 1e-06
highest = lax.Precision.HIGHEST

def objective(logits, expression, target, keep_flag, onehot, counts, kept_total):
    masked = jnp.where(keep_flag[:, None], logits, -1e+30)
    mapping = jax.nn.softmax(masked, axis=0)
    mapping_low = low(mapping)
    predicted = low_back(jnp.dot(expression.T, mapping_low, precision=highest))
    inner_prod = jnp.dot(predicted * target, onehot, precision=highest)
    predict_sq = jnp.dot(predicted * predicted, onehot, precision=highest)
    target_sq = jnp.dot(target * target, onehot, precision=highest)
    cosine = inner_prod * lax.rsqrt(predict_sq + norm_eps) * lax.rsqrt(target_sq + norm_eps)
    density = jnp.dot(mapping, onehot, precision=highest) / counts[None, :]
    log_density = jnp.log(jnp.where(keep_flag[:, None], density, 1.0))
    keep_weight = keep_flag.astype(jnp.float32)
    diverge = lax.optimization_barrier(jnp.sum(keep_weight[:, None] * (-jnp.log(kept_total) - log_density), axis=0)) / kept_total
    return (-jnp.sum(cosine) + density_weight * jnp.sum(diverge), predicted)

def reference(logits, expression, target, keep_mask, slide_ids, slide_counts):
    keep_flag = keep_mask > 0
    kept_total = jnp.sum(keep_flag.astype(jnp.float32))
    onehot = (slide_ids[:, None] == jnp.arange(NSLIDE, dtype=jnp.int32)[None, :]).astype(jnp.float32)
    counts = slide_counts.astype(jnp.float32)

    def wrapped(logit_arg, expression_arg):
        return objective(logit_arg, expression_arg, target, keep_flag, onehot, counts, kept_total)
    objective_value, pullback, predicted = jax.vjp(wrapped, logits, expression.astype(jnp.float32), has_aux=True)
    grad_logit, grad_expr = pullback(jnp.ones((), jnp.float32))
    mapping_loss = objective_value / (NSLIDE * NG)
    return (mapping_loss, predicted, kept_total * grad_logit, expression_scale * kept_total * grad_expr)
```

```python
import functools

import jax
import jax.numpy as jnp
from jax import lax
from jax.experimental import pallas as pl
from jax.experimental.pallas import tpu as pltpu
from jax.sharding import PartitionSpec as P

density_weight = 32.0
expression_scale = 64.0
norm_eps = 1e-06
f32 = jnp.float32
bf16 = jnp.bfloat16
VMEM_LIMIT = 56 << 20
COST_SHARE = 0.2
NT = (((1,), (1,)), ((), ()))
TN = (((0,), (0,)), ((), ()))


def cost(flops, bytes_accessed):
    return pl.CostEstimate(
        flops=int(flops * COST_SHARE),
        bytes_accessed=int(bytes_accessed * COST_SHARE),
        transcendentals=0,
    )


def params():
    return pltpu.CompilerParams(vmem_limit_bytes=VMEM_LIMIT)


def shape(dims, dtype):
    return jax.ShapeDtypeStruct(dims, dtype)


def dot(a, b, dims=(((1,), (0,)), ((), ()))):
    return lax.dot_general(a, b, dims, preferred_element_type=f32)


def halves(value):
    high = value.astype(bf16)
    return high, (value - high.astype(f32)).astype(bf16)


def thirds(value):
    high = value.astype(bf16)
    rest = value - high.astype(f32)
    middle = rest.astype(bf16)
    return high, middle, (rest - middle.astype(f32)).astype(bf16)


def split_rows(cells):
    unit = cells // 8
    return [unit, 2 * unit, 2 * unit, 2 * unit, unit]


def exp_call(logits, keep_rows, sums, whole, start, pieces_rows, final):
    cells, spots = logits.shape
    tile = 512
    first = start // tile
    counts = [size // tile for size in pieces_rows]
    begins = [sum(counts[:c]) for c in range(len(counts))]

    def body(x_ref, k_ref, *refs):
        if start:
            before_ref, refs = refs[0], refs[2:]
        piece_refs, (whole_ref, sum_ref) = refs[:-2], refs[-2:]
        step = pl.program_id(0)

        @pl.when(step == 0)
        def _():
            if start:
                sum_ref[...] = before_ref[...]
            else:
                sum_ref[...] = jnp.zeros_like(sum_ref)
            if final:
                kept = jnp.sum(k_ref[...].astype(f32)) * 0.125
                sum_ref[8:16, :] = jnp.full((8, spots), kept, f32)

        total = sum_ref[0:8, :]
        for g in range(tile // 128):
            row = (step + first) * (tile // 128) + g
            mask = jnp.broadcast_to(k_ref[pl.ds(row, 1), :].astype(f32), (128, 128)).T
            mask = jnp.concatenate([mask] * (spots // 128), axis=1)
            rise = jnp.exp(x_ref[g * 128 : (g + 1) * 128, :]) * mask
            whole_ref[g * 128 : (g + 1) * 128, :] = rise.astype(bf16)
            total = total + jnp.sum(rise.reshape(16, 8, spots), axis=0)
        sum_ref[0:8, :] = total
        for ref, begin, count in zip(piece_refs, begins, counts):

            @pl.when((step >= begin) & (step < begin + count))
            def _():
                ref[...] = whole_ref[...]

    def rows(c):
        return lambda i: (jnp.clip(i - begins[c], 0, counts[c] - 1), 0)

    in_specs = [
        pl.BlockSpec((tile, spots), lambda i: (i + first, 0)),
        pl.BlockSpec(keep_rows.shape, lambda i: (0, 0)),
    ]
    operands = [logits, keep_rows]
    aliases = {}
    if start:
        in_specs += [
            pl.BlockSpec((16, spots), lambda i: (0, 0)),
            pl.BlockSpec(memory_space=pl.ANY),
        ]
        operands += [sums, whole]
        aliases = {3: len(counts)}
    return pl.pallas_call(
        body,
        grid=(sum(counts),),
        in_specs=in_specs,
        out_specs=[pl.BlockSpec((tile, spots), rows(c)) for c in range(len(counts))]
        + [
            pl.BlockSpec((tile, spots), lambda i: (i + first, 0)),
            pl.BlockSpec((16, spots), lambda i: (0, 0)),
        ],
        out_shape=[shape((size, spots), bf16) for size in pieces_rows]
        + [shape((cells, spots), bf16), shape((16, spots), f32)],
        input_output_aliases=aliases,
        compiler_params=params(),
        cost_estimate=cost(0, 8 * sum(pieces_rows) * spots),
        name="exp_rows",
    )(*operands)


def part_call(expression, mapping, ids, picks, adds, dtypes):
    cells, spots = mapping.shape
    count = len(picks)
    block = expression.shape[1] // ids.shape[0]

    def body(ids_ref, *refs):
        e_refs, u_ref = refs[:count], refs[count]
        a_refs = refs[count + 1 : count + 1 + len(adds)]
        o_refs = refs[count + 1 + len(adds) :]
        both = jnp.concatenate([ref[...] for ref in e_refs], axis=1)
        terms = dot(both, u_ref[...], TN)
        for q in range(count):
            total = terms[q * block : (q + 1) * block, :]
            if q < len(adds):
                total = total + a_refs[q][...].astype(f32)
            o_refs[q][...] = total.astype(dtypes[q])

    def column(q):
        return lambda k, ids_ref: (0, ids_ref[q])

    flat = pl.BlockSpec((block, spots), lambda k, ids_ref: (0, 0))
    return pl.pallas_call(
        body,
        grid_spec=pltpu.PrefetchScalarGridSpec(
            num_scalar_prefetch=1,
            grid=(1,),
            in_specs=[pl.BlockSpec((cells, block), column(q)) for q in picks]
            + [pl.BlockSpec((cells, spots), lambda k, ids_ref: (0, 0))]
            + [flat] * len(adds),
            out_specs=[flat] * count,
        ),
        out_shape=[shape((block, spots), dtype) for dtype in dtypes],
        compiler_params=params(),
        cost_estimate=cost(
            2 * count * block * cells * spots, 2 * cells * (count * block + spots)
        ),
        name="part",
    )(ids, *[expression] * count, mapping, *adds)


def add_call(values):
    def body(*refs):
        total = refs[0][...].astype(f32)
        for ref in refs[1:-1]:
            total = total + ref[...].astype(f32)
        refs[-1][...] = total.astype(bf16)

    return pl.pallas_call(
        body,
        out_shape=shape(values[0].shape, bf16),
        compiler_params=params(),
        cost_estimate=cost(0, 8 * values[0].size),
        name="add_blocks",
    )(*values)


def total_of(tops_ref):
    return jnp.sum(tops_ref[0:8, :], axis=0, keepdims=True)


def kept_of(tops_ref):
    return jnp.sum(tops_ref[8:16, 0:1], axis=0, keepdims=True)


def predicted_call(values, tops, target, member):
    block, spots = target.shape
    slides = member.shape[0]

    def body(*refs):
        v_refs, (tops_ref, t_ref, m_ref, p_ref, s_ref) = refs[:-5], refs[-5:]
        total = v_refs[0][...].astype(f32)
        for ref in v_refs[1:]:
            total = total + ref[...].astype(f32)
        pred = total / total_of(tops_ref)
        p_ref[...] = pred
        target_now = t_ref[...]
        member_low = m_ref[...].astype(bf16)
        for q, value in enumerate((pred * target_now, pred * pred, target_now * target_now)):
            high, low = halves(value)
            s_ref[q * slides : (q + 1) * slides, :] = dot(member_low, high, NT) + dot(
                member_low, low, NT
            )

    return pl.pallas_call(
        body,
        out_shape=[shape((block, spots), f32), shape((3 * slides, block), f32)],
        compiler_params=params(),
        cost_estimate=cost(0, 16 * block * spots),
        name="predicted",
    )(*values, tops, target, member)


def grad_call(sums, far, pred, target, tops, member):
    block, spots = target.shape
    slides = member.shape[0]

    def body(s_ref, f_ref, p_ref, t_ref, tops_ref, m_ref, g_ref, e_ref):
        total = s_ref[...] + f_ref[...]
        inner = total[0:slides, :]
        inv_predict = lax.rsqrt(total[slides : 2 * slides, :] + norm_eps)
        inv_target = lax.rsqrt(total[2 * slides : 3 * slides, :] + norm_eps)
        pair = inv_predict * inv_target
        cosine = inner * pair
        member_low = m_ref[...].astype(bf16)
        pair_at = sum(dot(v, member_low, TN) for v in thirds(pair))
        curve_at = sum(dot(v, member_low, TN) for v in thirds(cosine * inv_predict * inv_predict))
        pred = p_ref[...]
        grad = (pred * curve_at - t_ref[...] * pair_at) / total_of(tops_ref)
        grad = grad.astype(bf16)
        g_ref[...] = grad
        column = jnp.sum(pred * grad.astype(f32), axis=0, keepdims=True)
        total = jnp.sum(jnp.sum(cosine, axis=1, keepdims=True), axis=0, keepdims=True)
        e_ref[...] = jnp.concatenate(
            [column, jnp.broadcast_to(total, (1, spots)), jnp.zeros((6, spots), f32)], axis=0
        )

    return pl.pallas_call(
        body,
        out_shape=[shape((block, spots), bf16), shape((8, spots), f32)],
        compiler_params=params(),
        cost_estimate=cost(0, 12 * block * spots),
        name="grad",
    )(sums, far, pred, target, tops, member)


def density_call(mapping, tops, member):
    cells, spots = mapping.shape
    slides = member.shape[0]
    tile = min(cells, 2048)

    def body(u_ref, tops_ref, m_ref, o_ref):
        high, low = halves(m_ref[...] / total_of(tops_ref))
        both = jnp.concatenate([high, low], axis=0)
        pad = jnp.zeros((128 - 2 * slides, spots), bf16)
        got = dot(u_ref[...], jnp.concatenate([both, pad], axis=0), NT).T
        o_ref[...] = got[0:slides, :] + got[slides : 2 * slides, :]

    return pl.pallas_call(
        body,
        grid=(cells // tile,),
        in_specs=[
            pl.BlockSpec((tile, spots), lambda i: (i, 0)),
            pl.BlockSpec((16, spots), lambda i: (0, 0)),
            pl.BlockSpec((slides, spots), lambda i: (0, 0)),
        ],
        out_specs=pl.BlockSpec((slides, tile), lambda i: (0, i)),
        out_shape=shape((slides, cells), f32),
        compiler_params=params(),
        cost_estimate=cost(0, 2 * cells * spots),
        name="density",
    )(mapping, tops, member)


def diverge_call(density, far, keep_line, counts, mapping, tops, member, ends):
    cells, spots = mapping.shape
    slides = member.shape[0]
    tile = min(cells, 2048)
    steps = cells // tile

    def body(d_ref, f_ref, k_ref, c_ref, u_ref, tops_ref, m_ref, ends_ref, o_ref, w_ref, e_ref, acc):
        step = pl.program_id(0)
        keep = k_ref[...].astype(f32)
        kept = kept_of(tops_ref)
        total = total_of(tops_ref)
        weight = m_ref[...] / total
        safe = jnp.where(keep > 0, d_ref[...] + f_ref[...], 1.0)
        slope = -density_weight * keep / (kept * safe)
        high, low = halves(slope)
        parts = jnp.concatenate([high, high, low, jnp.zeros_like(low)], axis=0)
        o_ref[...] = parts
        w_high, w_low = halves(weight)
        weights = jnp.concatenate([w_high, w_low, w_high, jnp.zeros_like(w_low)], axis=0)
        w_ref[...] = weights
        column = jnp.zeros((8, spots), f32)
        chunk = 256
        for r in range(tile // chunk):
            at = slice(r * chunk, (r + 1) * chunk)
            pulled = dot(parts[:, at], weights, TN) * u_ref[at, :].astype(f32)
            column += jnp.sum(pulled.reshape(chunk // 8, 8, spots), axis=0)
        logs = jnp.log(c_ref[...].astype(f32)) - jnp.log(kept) - jnp.log(safe)
        logs = jnp.sum(jnp.where(keep > 0, logs, 0.0), axis=1, keepdims=True)
        logs = jnp.sum(logs, axis=0, keepdims=True) / kept
        column = jnp.sum(column, axis=0, keepdims=True) / total

        @pl.when(step == 0)
        def _():
            acc[...] = ends_ref[...]

        acc[...] += jnp.concatenate(
            [
                column,
                jnp.zeros_like(column),
                jnp.broadcast_to(logs, (1, spots)),
                jnp.zeros((5, spots), f32),
            ],
            axis=0,
        )
        e_ref[...] = acc[...]

    return pl.pallas_call(
        body,
        grid=(steps,),
        in_specs=[
            pl.BlockSpec((slides, tile), lambda i: (0, i)),
            pl.BlockSpec((slides, tile), lambda i: (0, i)),
            pl.BlockSpec((1, tile), lambda i: (0, i)),
            pl.BlockSpec((slides, 1), lambda i: (0, 0)),
            pl.BlockSpec((tile, spots), lambda i: (i, 0)),
            pl.BlockSpec((16, spots), lambda i: (0, 0)),
            pl.BlockSpec((slides, spots), lambda i: (0, 0)),
            pl.BlockSpec((8, spots), lambda i: (0, 0)),
        ],
        out_specs=[
            pl.BlockSpec((4 * slides, tile), lambda i: (0, i)),
            pl.BlockSpec((4 * slides, spots), lambda i: (0, 0)),
            pl.BlockSpec((8, spots), lambda i: (0, 0)),
        ],
        out_shape=[
            shape((4 * slides, cells), bf16),
            shape((4 * slides, spots), bf16),
            shape((8, spots), f32),
        ],
        scratch_shapes=[pltpu.VMEM((8, spots), f32)],
        compiler_params=params(),
        cost_estimate=cost(0, 2 * cells * spots),
        name="diverge",
    )(density, far, keep_line, counts, mapping, tops, member, ends)


def regroup_call(blocks, ids, place, spread):
    count = len(blocks)
    block, spots = blocks[0].shape
    share = count * block // spread
    fars = spread // 2 - 1

    def body(ids_ref, place_ref, *refs):
        b_refs, o_refs = refs[:count], refs[count : count + 2 + fars]
        held, in_sem, out_sem = refs[count + 2 + fars :]
        here = place_ref[0]

        def rows(start, size):
            return held.at[pl.ds(pl.multiple_of(start, size), size)]

        copies = [
            pltpu.make_async_copy(b_refs[q], rows(ids_ref[q] * block, block), in_sem.at[q])
            for q in range(count)
        ]
        for copy in copies:
            copy.start()
        for copy in copies:
            copy.wait()
        copies = [
            pltpu.make_async_copy(
                rows(((here >> 1) ^ (w + 1)) * (2 * share), 2 * share),
                o_refs[2 + w],
                out_sem.at[2 + w],
            )
            for w in range(fars)
        ]
        copies += [
            pltpu.make_async_copy(rows((here ^ w) * share, share), o_refs[w], out_sem.at[w])
            for w in range(2)
        ]
        for copy in copies:
            copy.start()
        for copy in copies:
            copy.wait()

    smem = pl.BlockSpec(memory_space=pltpu.SMEM)
    anywhere = pl.BlockSpec(memory_space=pl.ANY)
    return pl.pallas_call(
        body,
        in_specs=[smem, smem] + [anywhere] * count,
        out_specs=[anywhere] * (2 + fars),
        out_shape=[shape((share, spots), bf16)] * 2 + [shape((2 * share, spots), bf16)] * fars,
        scratch_shapes=[
            pltpu.VMEM((count * block, spots), bf16),
            pltpu.SemaphoreType.DMA((count,)),
            pltpu.SemaphoreType.DMA((2 + fars,)),
        ],
        compiler_params=params(),
        cost_estimate=cost(0, 4 * count * block * spots),
        name="regroup",
    )(ids, place, *blocks)


def logit_call(expression, blocks, ids, mapping, slope, weight, ends, tops):
    cells, genes = expression.shape
    block, spots = blocks[0].shape
    count = len(blocks)
    tile = min(cells, 1024)

    def body(ids_ref, e_ref, u_ref, d_ref, w_ref, ends_ref, tops_ref, *refs):
        b_refs, (o_ref, held, sem) = refs[:count], refs[count:]

        @pl.when(pl.program_id(0) == 0)
        def _():
            copies = []
            for q in range(count):
                at = pl.ds(pl.multiple_of(ids_ref[q] * block, block), block)
                copies.append(pltpu.make_async_copy(b_refs[q], held.at[at], sem.at[q]))
            for copy in copies:
                copy.start()
            for copy in copies:
                copy.wait()

        acc = dot(e_ref[...], held[...])
        acc += dot(d_ref[...], w_ref[...], TN) - ends_ref[0:1, :]
        o_ref[...] = u_ref[...].astype(f32) * (acc * kept_of(tops_ref))

    return pl.pallas_call(
        body,
        grid=(cells // tile,),
        in_specs=[
            pl.BlockSpec(memory_space=pltpu.SMEM),
            pl.BlockSpec((tile, genes), lambda i: (i, 0)),
            pl.BlockSpec((tile, spots), lambda i: (i, 0)),
            pl.BlockSpec((slope.shape[0], tile), lambda i: (0, i)),
            pl.BlockSpec(weight.shape, lambda i: (0, 0)),
            pl.BlockSpec((8, spots), lambda i: (0, 0)),
            pl.BlockSpec((16, spots), lambda i: (0, 0)),
        ]
        + [pl.BlockSpec(memory_space=pl.ANY)] * count,
        out_specs=pl.BlockSpec((tile, spots), lambda i: (i, 0)),
        out_shape=shape((cells, spots), f32),
        scratch_shapes=[pltpu.VMEM((genes, spots), bf16), pltpu.SemaphoreType.DMA((count,))],
        compiler_params=params(),
        cost_estimate=cost(2 * cells * genes * spots, 2 * cells * genes + 6 * cells * spots),
        name="grad_logits",
    )(ids, expression, mapping, slope, weight, ends, tops, *blocks)


def expr_call(base, chunks, grads, tops, cells, start):
    spots = chunks[0][0].shape[1]
    genes = grads[0].shape[0]
    count = len(grads)
    tile = 512
    steps = [c[0].shape[0] // tile for c in chunks]
    begins = [sum(steps[:c]) for c in range(len(chunks))]
    first = start // tile

    def body(*refs):
        o_ref = refs[-1]
        g_refs = refs[len(chunks) * count : len(chunks) * count + count]
        tops_ref = refs[len(chunks) * count + count]
        step = pl.program_id(0)
        for c in range(len(chunks)):

            @pl.when((step >= begins[c]) & (step < begins[c] + steps[c]))
            def _():
                total = None
                for q in range(count):
                    term = dot(refs[c * count + q][...], g_refs[q][...], NT)
                    total = term if total is None else total + term
                o_ref[...] = total * (expression_scale * kept_of(tops_ref))

    def rows(c):
        return lambda i: (jnp.clip(i - begins[c], 0, steps[c] - 1), 0)

    in_specs = [pl.BlockSpec((tile, spots), rows(c)) for c in range(len(chunks)) for _ in range(count)]
    in_specs += [pl.BlockSpec((genes, spots), lambda i: (0, 0))] * count
    in_specs += [pl.BlockSpec((16, spots), lambda i: (0, 0))]
    operands = [v for c in chunks for v in c] + [*grads, tops]
    aliases = {}
    if base is not None:
        in_specs.append(pl.BlockSpec(memory_space=pl.ANY))
        operands.append(base)
        aliases = {len(operands) - 1: 0}
    rows_all = sum(steps) * tile
    return pl.pallas_call(
        body,
        grid=(sum(steps),),
        in_specs=in_specs,
        out_specs=pl.BlockSpec((tile, genes), lambda i: (i + first, 0)),
        out_shape=shape((cells, genes), f32),
        input_output_aliases=aliases,
        compiler_params=params(),
        cost_estimate=cost(
            2 * rows_all * spots * count * genes, 2 * rows_all * spots * count + 4 * rows_all * genes
        ),
        name="grad_expression",
    )(*operands)


def per_device(n, m, logits, expression, target, keep_mask, slide_ids, slide_counts):
    cells, spots = logits.shape
    genes = expression.shape[1]
    block = genes // n
    slide_total = slide_counts.shape[0]
    levels = n.bit_length() - 1
    lead = levels - 3
    orders = [[1 << k for k in range(levels)] for _ in range(2)]
    orders[1][0], orders[1][1] = 2, 1
    me = lax.axis_index("cell")
    place = lax.axis_index("spot")
    core = place & 1

    def across(value, k):
        pairs = [
            (i * m + j, (i ^ orders[j & 1][k]) * m + j) for i in range(n) for j in range(m)
        ]
        return lax.ppermute(value, ("cell", "spot"), pairs)

    def over_spot(value, mask):
        return lax.ppermute(value, "spot", [(j, j ^ mask) for j in range(m)])

    def over_cell(value, cell_mask, spot_mask):
        pairs = [
            (i * m + j, (i ^ cell_mask) * m + (j ^ spot_mask)) for i in range(n) for j in range(m)
        ]
        return lax.ppermute(value, ("cell", "spot"), pairs)

    def sum_cell(value):
        for k in range(levels):
            value = value + across(value, k)
        return value

    def sum_spot(value, aside):
        other = over_spot(value, 1)
        mask = 2
        while mask < m:
            value = value + other
            if aside:
                other = over_cell(over_cell(value, 1, 0), 1, mask)
            else:
                other = over_spot(value, mask)
            mask *= 2
        return value, other

    def tie(value, others):
        return lax.optimization_barrier((value, *others))[0]

    keep_rows = keep_mask.reshape(cells // 128, 128)
    sizes = split_rows(cells)
    starts = [sum(sizes[:c]) for c in range(len(sizes))]
    first, mapping, sums = exp_call(logits, keep_rows, None, None, 0, sizes[:1], False)
    *rest, mapping, sums = exp_call(logits, keep_rows, sums, mapping, sizes[0], sizes[1:], True)
    pieces = [first, *rest]
    gathered = []
    for piece in pieces:
        quarters = [None] * m
        for mask in range(0, m, 2):
            quarters[mask] = over_spot(piece, mask) if mask else piece
            quarters[mask + 1] = over_spot(quarters[mask], 1)
        gathered.append(quarters)

    def arrived(c):
        return [gathered[c][mask] for mask in range(2, m, 2)]

    tops = sum_cell(sums)

    def place_of(code):
        value = me
        for k in range(levels):
            if code[k]:
                value = value ^ jnp.where(core == 1, orders[1][k], orders[0][k])
        return value

    def codes(prefix):
        out = [prefix]
        while len(out[0]) < levels:
            out = [c + (b,) for c in out for b in (1, 0)]
        return out

    ids = jnp.stack([place_of(c) for c in codes(())])
    order = {c[lead:]: q for q, c in enumerate(codes((0,) * lead))}

    def products(first, second, adds, dtypes):
        return part_call(expression, mapping, ids, [order[first], order[second]], adds, dtypes)

    part, got, step = {}, {}, {}
    if lead or block % 128:
        have = dot(expression, mapping, TN).reshape(n, block, spots)
        have = jnp.take(have, ids, axis=0)
        for k in range(lead):
            half = have.shape[0] // 2
            have = have[half:] + across(have[:half].astype(bf16), k).astype(f32)
        for code, q in order.items():
            part[code] = have[q]
        for a in (1, 0):
            for b in (1, 0):
                got[1, a, b] = across(part[1, a, b].astype(bf16), lead)
        for b in (1, 0):
            part[0, 1, b] = add_call([part[0, 1, b], got[1, 1, b]])
            step[0, 1, b] = across(part[0, 1, b], lead + 1)
        adds = [part[0, 0, 0], got[1, 0, 0]]
    else:
        part[1, 1, 1], part[1, 0, 1] = products((1, 1, 1), (1, 0, 1), [], [bf16] * 2)
        got[1, 1, 1], got[1, 0, 1] = across(part[1, 1, 1], 0), across(part[1, 0, 1], 0)
        got[1, 1, 1] = tie(got[1, 1, 1], arrived(0))
        part[0, 1, 1], part[0, 0, 1] = products(
            (0, 1, 1), (0, 0, 1), [got[1, 1, 1]], [bf16, f32]
        )
        step[0, 1, 1] = across(part[0, 1, 1], 1)
        part[1, 1, 0], part[1, 0, 0] = products((1, 1, 0), (1, 0, 0), [], [bf16] * 2)
        got[1, 1, 0], got[1, 0, 0] = across(part[1, 1, 0], 0), across(part[1, 0, 0], 0)
        part[0, 1, 0], part[0, 0, 0] = products(
            (0, 1, 0), (0, 0, 0), [got[1, 1, 0], got[1, 0, 0]], [bf16, f32]
        )
        step[0, 1, 0] = across(part[0, 1, 0], 1)
        adds = [part[0, 0, 0]]
    last = add_call([part[0, 0, 1], got[1, 0, 1], step[0, 1, 1]])
    last = across(last, lead + 2)

    slides = jnp.arange(slide_total, dtype=jnp.int32)
    member = (slide_ids[None, :] == slides[:, None]).astype(f32)
    last = tie(last, arrived(1))
    predicted, gene_sums = predicted_call(
        [*adds, step[0, 1, 0], last], tops, target, member
    )
    gene_sums, far_sums = sum_spot(gene_sums, True)
    far_sums = tie(far_sums, arrived(2))
    grad, ends = grad_call(gene_sums, far_sums, predicted, target, tops, member)

    have = {(0, 0, 0): grad}
    for k in (2, 1, 0):
        for code in list(have):
            other = tuple(1 if q == k else b for q, b in enumerate(code))
            have[other] = across(have[code], lead + k)
    tail = codes((0,) * lead)
    blocks = [have[c[lead:]] for c in tail]
    if lead:
        blocks = jnp.stack(blocks)
        for k in reversed(range(lead)):
            blocks = jnp.concatenate([across(blocks, k), blocks])
        blocks = [blocks[q] for q in range(n)]

    density, far_density = sum_spot(density_call(mapping, tops, member), False)
    slope, weight, ends = diverge_call(
        density,
        far_density,
        keep_mask[None, :],
        slide_counts[:, None],
        mapping,
        tops,
        member,
        ends,
    )
    ends = sum_cell(ends)
    mapping_loss = (-ends[1, 0] + density_weight * ends[2, 0]) / (slide_total * genes)

    mine, beside, *far = regroup_call(blocks, ids, place[None], m)
    grad_logits = logit_call(
        expression, blocks, ids, mapping, slope, weight, tie(ends, arrived(3)), tops
    )
    share = genes // m
    regrouped = [None] * m
    regrouped[0], regrouped[1] = mine, over_spot(beside, 1)
    for q, pair in enumerate(far):
        mask = 2 * (q + 1)
        pair = over_spot(pair, mask).reshape(2, share, spots)
        regrouped[mask] = lax.dynamic_index_in_dim(pair, core, 0, keepdims=False)
        regrouped[mask + 1] = over_spot(
            lax.dynamic_index_in_dim(pair, 1 - core, 0, keepdims=False), 1
        )
    grad_expression = expr_call(None, gathered[:-1], regrouped, tops, cells, 0)
    grad_expression = expr_call(
        grad_expression, gathered[-1:], regrouped, tops, cells, starts[-1]
    )
    return (mapping_loss, predicted, grad_logits, grad_expression)


def solution(mesh):
    in_specs = (P("cell", "spot"), P("cell", None), P("cell", "spot"), P("cell"), P("spot"), P())
    out_specs = (P(), P("cell", "spot"), P("cell", "spot"), P("cell", "spot"))
    body = functools.partial(per_device, mesh.shape["cell"], mesh.shape["spot"])
    return jax.shard_map(
        body, mesh=mesh, in_specs=in_specs, out_specs=out_specs, check_vma=False
    )
```

```python
import functools

import jax
import jax.numpy as jnp
from jax import lax
from jax.experimental import pallas as pl
from jax.experimental.pallas import tpu as pltpu
from jax.sharding import PartitionSpec as P

density_weight = 32.0
expression_scale = 64.0
norm_eps = 1e-06
f32 = jnp.float32
bf16 = jnp.bfloat16
VMEM_LIMIT = 16 << 20
COST_SHARE = 1.0
NT = (((1,), (1,)), ((), ()))
TN = (((0,), (0,)), ((), ()))


def cost(flops, bytes_accessed):
    return pl.CostEstimate(
        flops=int(flops * COST_SHARE),
        bytes_accessed=int(bytes_accessed * COST_SHARE),
        transcendentals=0,
    )


ANY = pl.BlockSpec(memory_space=pl.ANY)
HBM = pl.BlockSpec(memory_space=pltpu.HBM)
VMEM = pl.BlockSpec(memory_space=pltpu.VMEM)
SMEM = pl.BlockSpec(memory_space=pltpu.SMEM)


def params():
    return pltpu.CompilerParams(vmem_limit_bytes=VMEM_LIMIT)


def shape(dims, dtype):
    return jax.ShapeDtypeStruct(dims, dtype)


def dot(a, b, dims=(((1,), (0,)), ((), ()))):
    return lax.dot_general(a, b, dims, preferred_element_type=f32)


def halves(value):
    high = value.astype(bf16)
    return high, (value - high.astype(f32)).astype(bf16)


def thirds(value):
    high = value.astype(bf16)
    rest = value - high.astype(f32)
    middle = rest.astype(bf16)
    return high, middle, (rest - middle.astype(f32)).astype(bf16)


def split_rows(cells):
    unit = cells // 8
    return [unit, 2 * unit, 2 * unit, 2 * unit, unit]


def column_mask(k_ref, group, spots):
    line = jnp.broadcast_to(k_ref[group : group + 1, :].astype(f32), (128, 128)).T
    return jnp.concatenate([line] * (spots // 128), axis=1)


def in_hbm(value):
    return pltpu.with_memory_space_constraint(value, pltpu.HBM)


def first_call(logits, keep_rows, size):
    spots = logits.shape[1]

    def body(x_ref, k_ref, o_ref, x_buf, sem):
        copy = pltpu.make_async_copy(x_ref.at[pl.ds(0, size)], x_buf, sem)
        copy.start()
        copy.wait()
        for g in range(size // 128):
            at = slice(g * 128, (g + 1) * 128)
            o_ref[at, :] = (jnp.exp(x_buf[at, :]) * column_mask(k_ref, g, spots)).astype(bf16)

    return pl.pallas_call(
        body,
        in_specs=[HBM, VMEM],
        out_specs=VMEM,
        out_shape=shape((size, spots), bf16),
        scratch_shapes=[pltpu.VMEM((size, spots), f32), pltpu.SemaphoreType.DMA],
        compiler_params=params(),
        cost_estimate=cost(0, 6 * size * spots),
        name="exp_first",
    )(in_hbm(logits), keep_rows)


def exp_call(logits, keep_rows, sizes):
    cells, spots = logits.shape
    tile = 512
    steps = cells // tile
    starts = [sum(sizes[:c]) for c in range(len(sizes))]

    def body(x_ref, k_ref, *refs):
        piece_refs = (None, *refs[: len(sizes) - 1])
        u_ref, s_ref, x_buf, sem, p_sem = refs[len(sizes) - 1 :]
        fetch = [
            pltpu.make_async_copy(
                x_ref.at[pl.ds(t * tile, tile)], x_buf.at[pl.ds(t * tile, tile)], sem.at[t]
            )
            for t in range(steps)
        ]
        for copy in fetch:
            copy.start()
        total = jnp.zeros((8, spots), f32)
        sent = []
        for t in range(steps):
            fetch[t].wait()
            for g in range(tile // 128):
                at = slice(t * tile + g * 128, t * tile + (g + 1) * 128)
                rise = jnp.exp(x_buf[at, :])
                rise = rise * column_mask(k_ref, t * (tile // 128) + g, spots)
                u_ref[at, :] = rise.astype(bf16)
                total = total + jnp.sum(rise.reshape(16, 8, spots), axis=0)
            for c in range(1, len(sizes)):
                if starts[c] + sizes[c] == (t + 1) * tile:
                    copy = pltpu.make_async_copy(
                        u_ref.at[pl.ds(starts[c], sizes[c])], piece_refs[c], p_sem.at[c]
                    )
                    copy.start()
                    sent.append(copy)
        s_ref[0:8, :] = total
        kept = jnp.sum(k_ref[...].astype(f32)) * 0.125
        s_ref[8:16, :] = jnp.full((8, spots), kept, f32)
        for copy in sent:
            copy.wait()

    return pl.pallas_call(
        body,
        in_specs=[HBM, VMEM],
        out_specs=[HBM] * (len(sizes) - 1) + [VMEM] * 2,
        out_shape=[pltpu.HBM((size, spots), bf16) for size in sizes[1:]]
        + [shape((cells, spots), bf16), shape((16, spots), f32)],
        scratch_shapes=[
            pltpu.VMEM((cells, spots), f32),
            pltpu.SemaphoreType.DMA((steps,)),
            pltpu.SemaphoreType.DMA((len(sizes),)),
        ],
        compiler_params=params(),
        cost_estimate=cost(0, 8 * cells * spots),
        name="exp_rows",
    )(in_hbm(logits), keep_rows)


def part_call(expression, mapping, ids, picks, adds, dtypes):
    cells, spots = mapping.shape
    count = len(picks)
    block = expression.shape[1] // ids.shape[0]

    def body(ids_ref, e_ref, u_ref, *refs):
        a_refs, o_refs = refs[: len(adds)], refs[len(adds) : len(adds) + count]
        held, sem = refs[len(adds) + count :]
        copies = []
        for q, pick in enumerate(picks):
            at = pl.ds(pl.multiple_of(ids_ref[pick] * block, block), block)
            copies.append(pltpu.make_async_copy(e_ref.at[:, at], held.at[q], sem.at[q]))
            copies[q].start()
        for q in range(count):
            copies[q].wait()
            total = dot(held[q], u_ref[...], TN)
            if q < len(adds):
                total = total + a_refs[q][...].astype(f32)
            o_refs[q][...] = total.astype(dtypes[q])

    return pl.pallas_call(
        body,
        in_specs=[SMEM, HBM, VMEM] + [VMEM] * len(adds),
        out_specs=[VMEM] * count,
        out_shape=[shape((block, spots), dtype) for dtype in dtypes],
        scratch_shapes=[
            pltpu.VMEM((count, cells, block), bf16),
            pltpu.SemaphoreType.DMA((count,)),
        ],
        compiler_params=params(),
        cost_estimate=cost(
            2 * count * block * cells * spots, 2 * cells * (count * block + spots)
        ),
        name="part",
    )(ids, in_hbm(expression), mapping, *adds)


def add_call(values):
    def body(*refs):
        total = refs[0][...].astype(f32)
        for ref in refs[1:-1]:
            total = total + ref[...].astype(f32)
        refs[-1][...] = total.astype(bf16)

    return pl.pallas_call(
        body,
        out_shape=shape(values[0].shape, bf16),
        compiler_params=params(),
        cost_estimate=cost(0, 8 * values[0].size),
        name="add_blocks",
    )(*values)


def total_of(tops_ref):
    return jnp.sum(tops_ref[0:8, :], axis=0, keepdims=True)


def kept_of(tops_ref):
    return jnp.sum(tops_ref[8:16, 0:1], axis=0, keepdims=True)


def predicted_call(values, tops, target, member):
    block, spots = target.shape
    slides = member.shape[0]

    def body(*refs):
        v_refs, (tops_ref, t_ref, m_ref, p_ref, s_ref) = refs[:-5], refs[-5:]
        total = v_refs[0][...].astype(f32)
        for ref in v_refs[1:]:
            total = total + ref[...].astype(f32)
        pred = total / total_of(tops_ref)
        p_ref[...] = pred
        target_now = t_ref[...]
        member_low = m_ref[...].astype(bf16)
        for q, value in enumerate((pred * target_now, pred * pred, target_now * target_now)):
            high, low = halves(value)
            s_ref[q * slides : (q + 1) * slides, :] = dot(member_low, high, NT) + dot(
                member_low, low, NT
            )

    return pl.pallas_call(
        body,
        out_shape=[shape((block, spots), f32), shape((3 * slides, block), f32)],
        compiler_params=params(),
        cost_estimate=cost(0, 16 * block * spots),
        name="predicted",
    )(*values, tops, target, member)


def grad_call(sums, far, pred, target, tops, member):
    block, spots = target.shape
    slides = member.shape[0]

    def body(s_ref, f_ref, p_ref, t_ref, tops_ref, m_ref, g_ref, e_ref):
        total = s_ref[...] + f_ref[...]
        inner = total[0:slides, :]
        inv_predict = lax.rsqrt(total[slides : 2 * slides, :] + norm_eps)
        inv_target = lax.rsqrt(total[2 * slides : 3 * slides, :] + norm_eps)
        pair = inv_predict * inv_target
        cosine = inner * pair
        member_low = m_ref[...].astype(bf16)
        pair_at = sum(dot(v, member_low, TN) for v in thirds(pair))
        curve_at = sum(dot(v, member_low, TN) for v in thirds(cosine * inv_predict * inv_predict))
        pred = p_ref[...]
        grad = (pred * curve_at - t_ref[...] * pair_at) / total_of(tops_ref)
        grad = grad.astype(bf16)
        g_ref[...] = grad
        column = jnp.sum(pred * grad.astype(f32), axis=0, keepdims=True)
        total = jnp.sum(jnp.sum(cosine, axis=1, keepdims=True), axis=0, keepdims=True)
        e_ref[...] = jnp.concatenate(
            [column, jnp.broadcast_to(total, (1, spots)), jnp.zeros((6, spots), f32)], axis=0
        )

    return pl.pallas_call(
        body,
        out_shape=[shape((block, spots), bf16), shape((8, spots), f32)],
        compiler_params=params(),
        cost_estimate=cost(0, 12 * block * spots),
        name="grad",
    )(sums, far, pred, target, tops, member)


def density_call(mapping, tops, member):
    cells, spots = mapping.shape
    slides = member.shape[0]
    tile = min(cells, 1024)

    def body(u_ref, tops_ref, m_ref, o_ref):
        high, low = halves(m_ref[...] / total_of(tops_ref))
        pad = jnp.zeros((128 - 2 * slides, spots), bf16)
        both = jnp.concatenate([high, low, pad], axis=0)
        for t in range(cells // tile):
            at = slice(t * tile, (t + 1) * tile)
            got = dot(u_ref[at, :], both, NT).T
            o_ref[:, at] = got[0:slides, :] + got[slides : 2 * slides, :]

    return pl.pallas_call(
        body,
        in_specs=[VMEM] * 3,
        out_specs=VMEM,
        out_shape=shape((slides, cells), f32),
        compiler_params=params(),
        cost_estimate=cost(0, 2 * cells * spots),
        name="density",
    )(mapping, tops, member)


def diverge_call(density, far, keep_line, counts, mapping, tops, member):
    cells, spots = mapping.shape
    slides = member.shape[0]

    def body(d_ref, f_ref, k_ref, c_ref, u_ref, tops_ref, m_ref, o_ref, w_ref, e_ref):
        keep = k_ref[...].astype(f32)
        kept = kept_of(tops_ref)
        total = total_of(tops_ref)
        safe = jnp.where(keep > 0, d_ref[...] + f_ref[...], 1.0)
        high, low = halves(-density_weight * keep / (kept * safe))
        o_ref[...] = jnp.concatenate([high, high, low, jnp.zeros_like(low)], axis=0)
        w_high, w_low = halves(m_ref[...] / total)
        w_ref[...] = jnp.concatenate([w_high, w_low, w_high, jnp.zeros_like(w_low)], axis=0)
        column = jnp.zeros((8, spots), f32)
        chunk = 256
        for r in range(cells // chunk):
            at = slice(r * chunk, (r + 1) * chunk)
            pulled = dot(o_ref[:, at], w_ref[...], TN) * u_ref[at, :].astype(f32)
            column += jnp.sum(pulled.reshape(chunk // 8, 8, spots), axis=0)
        column = jnp.sum(column, axis=0, keepdims=True) / total
        logs = jnp.sum(jnp.log(safe), axis=0, keepdims=True)
        logs = -jnp.sum(logs, axis=1, keepdims=True)
        scale = jnp.sum(jnp.log(c_ref[...].astype(f32)), axis=1, keepdims=True)
        scale = scale - slides * jnp.log(kept)
        diverge = (logs + scale * jnp.sum(keep, axis=1, keepdims=True)) / kept
        e_ref[...] = jnp.concatenate(
            [
                column,
                jnp.zeros_like(column),
                jnp.broadcast_to(diverge, (1, spots)),
                jnp.zeros((5, spots), f32),
            ],
            axis=0,
        )

    return pl.pallas_call(
        body,
        in_specs=[VMEM] * 7,
        out_specs=[VMEM] * 3,
        out_shape=[
            shape((4 * slides, cells), bf16),
            shape((4 * slides, spots), bf16),
            shape((8, spots), f32),
        ],
        compiler_params=params(),
        cost_estimate=cost(0, 2 * cells * spots),
        name="diverge",
    )(density, far, keep_line, counts, mapping, tops, member)


def regroup_call(blocks, ids, place, spread):
    count = len(blocks)
    block, spots = blocks[0].shape
    share = count * block // spread

    def body(ids_ref, place_ref, *refs):
        b_refs, o_refs = refs[:count], refs[count : count + spread]
        held, in_sem, out_sem = refs[count + spread :]

        def rows(start, size):
            return held.at[pl.ds(pl.multiple_of(start, size), size)]

        copies = [
            pltpu.make_async_copy(b_refs[q], rows(ids_ref[q] * block, block), in_sem.at[q])
            for q in range(count)
        ]
        for copy in copies:
            copy.start()
        for copy in copies:
            copy.wait()
        copies = [
            pltpu.make_async_copy(rows((place_ref[0] ^ w) * share, share), o_refs[w], out_sem.at[w])
            for w in range(spread)
        ]
        for copy in copies:
            copy.start()
        for copy in copies:
            copy.wait()

    return pl.pallas_call(
        body,
        in_specs=[SMEM, SMEM] + [ANY] * count,
        out_specs=[HBM] * spread,
        out_shape=[shape((share, spots), bf16)] * spread,
        scratch_shapes=[
            pltpu.VMEM((count * block, spots), bf16),
            pltpu.SemaphoreType.DMA((count,)),
            pltpu.SemaphoreType.DMA((spread,)),
        ],
        compiler_params=params(),
        cost_estimate=cost(0, 4 * count * block * spots),
        name="regroup",
    )(ids, place, *blocks)


def logit_call(expression, blocks, ids, mapping, slope, weight, ends, tops):
    cells, genes = expression.shape
    block, spots = blocks[0].shape
    count = len(blocks)
    tile = min(cells, 1024)

    def body(ids_ref, e_ref, u_ref, d_ref, w_ref, ends_ref, tops_ref, *refs):
        b_refs, (o_ref, held, sem) = refs[:count], refs[count:]

        @pl.when(pl.program_id(0) == 0)
        def _():
            copies = []
            for q in range(count):
                at = pl.ds(pl.multiple_of(ids_ref[q] * block, block), block)
                copies.append(pltpu.make_async_copy(b_refs[q], held.at[at], sem.at[q]))
            for copy in copies:
                copy.start()
            for copy in copies:
                copy.wait()

        at = pl.ds(pl.multiple_of(pl.program_id(0) * tile, tile), tile)
        acc = dot(e_ref[at, :], held[...])
        acc += dot(d_ref[...], w_ref[...], TN) - ends_ref[0:1, :]
        o_ref[...] = u_ref[at, :].astype(f32) * (acc * kept_of(tops_ref))

    return pl.pallas_call(
        body,
        grid=(cells // tile,),
        in_specs=[SMEM, VMEM, VMEM, pl.BlockSpec((slope.shape[0], tile), lambda i: (0, i))]
        + [VMEM] * 3
        + [ANY] * count,
        out_specs=pl.BlockSpec((tile, spots), lambda i: (i, 0)),
        out_shape=shape((cells, spots), f32),
        scratch_shapes=[pltpu.VMEM((genes, spots), bf16), pltpu.SemaphoreType.DMA((count,))],
        compiler_params=params(),
        cost_estimate=cost(2 * cells * genes * spots, 2 * cells * genes + 6 * cells * spots),
        name="grad_logits",
    )(ids, expression, mapping, slope, weight, ends, tops, *blocks)


def expr_call(base, mapping, chunks, grads, tops, start):
    cells, spots = mapping.shape
    genes = grads[0].shape[0]
    count = len(grads)
    tile = 512
    tiles = [(c, t) for c in range(len(chunks)) for t in range(chunks[c][0].shape[0] // tile)]
    slots = min(3, len(tiles))
    flat = [v for chunk in chunks for v in chunk]

    def body(*refs):
        q_refs = refs[: len(flat)]
        u_ref = refs[len(flat)]
        g_refs = refs[len(flat) + 1 : len(flat) + 1 + count]
        tops_ref = refs[len(flat) + 1 + count]
        o_ref, held, out, in_sem, out_sem = refs[-5:]
        scale = expression_scale * kept_of(tops_ref)

        def fetch(k):
            c, t = tiles[k]
            return [
                pltpu.make_async_copy(
                    q_refs[c * (count - 1) + q].at[pl.ds(t * tile, tile)],
                    held.at[k % slots, q],
                    in_sem.at[k % slots, q],
                )
                for q in range(count - 1)
            ]

        def store(k):
            return pltpu.make_async_copy(
                out.at[k % 2], o_ref.at[pl.ds(start + k * tile, tile)], out_sem.at[k % 2]
            )

        for k in range(slots):
            for copy in fetch(k):
                copy.start()
        for k in range(len(tiles)):
            at = slice(start + k * tile, start + (k + 1) * tile)
            total = dot(u_ref[at, :], g_refs[0][...], NT)
            for copy in fetch(k):
                copy.wait()
            for q in range(1, count):
                total = total + dot(held[k % slots, q - 1], g_refs[q][...], NT)
            if k >= 2:
                store(k - 2).wait()
            out[k % 2] = total * scale
            store(k).start()
            if k + slots < len(tiles):
                for copy in fetch(k + slots):
                    copy.start()
        for k in range(max(len(tiles) - 2, 0), len(tiles)):
            store(k).wait()

    operands = [*flat, mapping, *grads, tops]
    in_specs = [ANY] * len(flat) + [VMEM] * (count + 2)
    aliases = {}
    if base is not None:
        in_specs.append(HBM)
        operands.append(base)
        aliases = {len(operands) - 1: 0}
    rows = len(tiles) * tile
    return pl.pallas_call(
        body,
        in_specs=in_specs,
        out_specs=HBM,
        out_shape=shape((cells, genes), f32),
        input_output_aliases=aliases,
        scratch_shapes=[
            pltpu.VMEM((slots, count - 1, tile, spots), bf16),
            pltpu.VMEM((2, tile, genes), f32),
            pltpu.SemaphoreType.DMA((slots, count - 1)),
            pltpu.SemaphoreType.DMA((2,)),
        ],
        compiler_params=params(),
        cost_estimate=cost(
            2 * rows * spots * count * genes, 2 * rows * spots * count + 4 * rows * genes
        ),
        name="grad_expression",
    )(*operands)


def per_device(n, m, logits, expression, target, keep_mask, slide_ids, slide_counts):
    cells, spots = logits.shape
    genes = expression.shape[1]
    block = genes // n
    slide_total = slide_counts.shape[0]
    levels = n.bit_length() - 1
    lead = levels - 3
    orders = [[1 << k for k in range(levels)] for _ in range(2)]
    orders[1][0], orders[1][1] = 2, 1
    me = lax.axis_index("cell")
    place = lax.axis_index("spot")
    core = place & 1

    def across(value, k):
        pairs = [
            (i * m + j, (i ^ orders[j & 1][k]) * m + j) for i in range(n) for j in range(m)
        ]
        return lax.ppermute(value, ("cell", "spot"), pairs)

    def over_spot(value, mask):
        return lax.ppermute(value, "spot", [(j, j ^ mask) for j in range(m)])

    def over_cell(value, cell_mask, spot_mask):
        pairs = [
            (i * m + j, (i ^ cell_mask) * m + (j ^ spot_mask)) for i in range(n) for j in range(m)
        ]
        return lax.ppermute(value, ("cell", "spot"), pairs)

    def sum_cell(value):
        for k in range(levels):
            value = value + across(value, k)
        return value

    def sum_spot(value, aside):
        other = over_spot(value, 1)
        mask = 2
        while mask < m:
            value = value + other
            if aside:
                other = over_cell(over_cell(value, 1, 0), 1, mask)
            else:
                other = over_spot(value, mask)
            mask *= 2
        return value, other

    def tie(value, others):
        return lax.optimization_barrier((value, *others))[0]

    keep_rows = keep_mask.reshape(cells // 128, 128)
    sizes = split_rows(cells)
    starts = [sum(sizes[:c]) for c in range(len(sizes))]
    pieces = [first_call(logits, keep_rows, sizes[0])]
    *rest, mapping, sums = exp_call(logits, keep_rows, sizes)
    pieces += rest
    gathered = []
    for piece in pieces:
        quarters = [None] * m
        for mask in range(0, m, 2):
            quarters[mask] = over_spot(piece, mask) if mask else piece
            quarters[mask + 1] = over_spot(quarters[mask], 1)
        gathered.append(quarters)

    def arrived(c):
        return [gathered[c][mask] for mask in range(2, m, 2)]

    tops = sum_cell(sums)

    def place_of(code):
        value = me
        for k in range(levels):
            if code[k]:
                value = value ^ jnp.where(core == 1, orders[1][k], orders[0][k])
        return value

    def codes(prefix):
        out = [prefix]
        while len(out[0]) < levels:
            out = [c + (b,) for c in out for b in (1, 0)]
        return out

    ids = jnp.stack([place_of(c) for c in codes(())])
    order = {c[lead:]: q for q, c in enumerate(codes((0,) * lead))}

    def products(first, second, adds, dtypes):
        return part_call(expression, mapping, ids, [order[first], order[second]], adds, dtypes)

    part, got, step = {}, {}, {}
    if lead or block % 128:
        have = dot(expression, mapping, TN).reshape(n, block, spots)
        have = jnp.take(have, ids, axis=0)
        for k in range(lead):
            half = have.shape[0] // 2
            have = have[half:] + across(have[:half].astype(bf16), k).astype(f32)
        for code, q in order.items():
            part[code] = have[q]
        for a in (1, 0):
            for b in (1, 0):
                got[1, a, b] = across(part[1, a, b].astype(bf16), lead)
        for b in (1, 0):
            part[0, 1, b] = add_call([part[0, 1, b], got[1, 1, b]])
            step[0, 1, b] = across(part[0, 1, b], lead + 1)
        adds = [part[0, 0, 0], got[1, 0, 0]]
    else:
        part[1, 1, 1], part[1, 0, 1] = products((1, 1, 1), (1, 0, 1), [], [bf16] * 2)
        got[1, 1, 1], got[1, 0, 1] = across(part[1, 1, 1], 0), across(part[1, 0, 1], 0)
        got[1, 1, 1] = tie(got[1, 1, 1], arrived(0))
        part[0, 1, 1], part[0, 0, 1] = products(
            (0, 1, 1), (0, 0, 1), [got[1, 1, 1]], [bf16, f32]
        )
        step[0, 1, 1] = across(part[0, 1, 1], 1)
        part[1, 1, 0], part[1, 0, 0] = products((1, 1, 0), (1, 0, 0), [], [bf16] * 2)
        got[1, 1, 0], got[1, 0, 0] = across(part[1, 1, 0], 0), across(part[1, 0, 0], 0)
        part[0, 1, 0], part[0, 0, 0] = products(
            (0, 1, 0), (0, 0, 0), [got[1, 1, 0], got[1, 0, 0]], [bf16, f32]
        )
        step[0, 1, 0] = across(part[0, 1, 0], 1)
        adds = [part[0, 0, 0]]
    last = add_call([part[0, 0, 1], got[1, 0, 1], step[0, 1, 1]])
    last = across(last, lead + 2)

    slides = jnp.arange(slide_total, dtype=jnp.int32)
    member = (slide_ids[None, :] == slides[:, None]).astype(f32)
    density, far_density = sum_spot(density_call(mapping, tops, member), True)
    last = tie(last, [*arrived(1), density])
    predicted, gene_sums = predicted_call(
        [*adds, step[0, 1, 0], last], tops, target, member
    )
    gene_sums, far_sums = sum_spot(gene_sums, True)
    far_sums = tie(far_sums, arrived(2))
    grad, ends = grad_call(gene_sums, far_sums, predicted, target, tops, member)

    slope, weight, more = diverge_call(
        density,
        far_density,
        keep_mask[None, :],
        slide_counts[None, :],
        mapping,
        tops,
        member,
    )
    ends = sum_cell(ends + more)
    mapping_loss = (-ends[1, 0] + density_weight * ends[2, 0]) / (slide_total * genes)

    have = {(0, 0, 0): grad}
    for k in (2, 1, 0):
        for code in list(have):
            other = tuple(1 if q == k else b for q, b in enumerate(code))
            source = tie(have[code], [slope]) if (k, code) == (0, (0, 1, 1)) else have[code]
            have[other] = across(source, lead + k)
    tail = codes((0,) * lead)
    blocks = [have[c[lead:]] for c in tail]
    if lead:
        blocks = jnp.stack(blocks)
        for k in reversed(range(lead)):
            blocks = jnp.concatenate([across(blocks, k), blocks])
        blocks = [blocks[q] for q in range(n)]

    grad_logits = logit_call(
        expression, blocks, ids, mapping, slope, weight, tie(ends, arrived(3)), tops
    )

    parts = regroup_call(blocks, ids, place[None], m)
    regrouped = [None] * m
    for mask in range(0, m, 2):
        regrouped[mask] = over_spot(parts[mask], mask) if mask else parts[0]
        beside = over_spot(parts[mask + 1], mask) if mask else parts[1]
        regrouped[mask + 1] = over_spot(beside, 1)
    chunks = [quarters[1:] for quarters in gathered]
    grad_expression = expr_call(None, mapping, chunks[:-1], regrouped, tops, 0)
    grad_expression = expr_call(
        grad_expression, mapping, chunks[-1:], regrouped, tops, starts[-1]
    )
    return (mapping_loss, predicted, grad_logits, grad_expression)


def solution(mesh):
    in_specs = (P("cell", "spot"), P("cell", None), P("cell", "spot"), P("cell"), P("spot"), P())
    out_specs = (P(), P("cell", "spot"), P("cell", "spot"), P("cell", "spot"))
    body = functools.partial(per_device, mesh.shape["cell"], mesh.shape["spot"])
    return jax.shard_map(
        body, mesh=mesh, in_specs=in_specs, out_specs=out_specs, check_vma=False
    )
```

```python
import functools

import jax
import jax.numpy as jnp
from jax import lax
from jax.experimental import pallas as pl
from jax.experimental.pallas import tpu as pltpu
from jax.sharding import PartitionSpec as P

density_weight = 32.0
expression_scale = 64.0
norm_eps = 1e-06
f32 = jnp.float32
bf16 = jnp.bfloat16
VMEM_LIMIT = 16 << 20
COST_SHARE = 0.05
NT = (((1,), (1,)), ((), ()))
TN = (((0,), (0,)), ((), ()))


def cost(flops, bytes_accessed):
    return pl.CostEstimate(
        flops=int(flops * COST_SHARE),
        bytes_accessed=int(bytes_accessed * COST_SHARE),
        transcendentals=0,
    )


ANY = pl.BlockSpec(memory_space=pl.ANY)
HBM = pl.BlockSpec(memory_space=pltpu.HBM)
VMEM = pl.BlockSpec(memory_space=pltpu.VMEM)
SMEM = pl.BlockSpec(memory_space=pltpu.SMEM)


def params():
    return pltpu.CompilerParams(vmem_limit_bytes=VMEM_LIMIT)


def shape(dims, dtype):
    return jax.ShapeDtypeStruct(dims, dtype)


def dot(a, b, dims=(((1,), (0,)), ((), ()))):
    return lax.dot_general(a, b, dims, preferred_element_type=f32)


def halves(value):
    high = value.astype(bf16)
    return high, (value - high.astype(f32)).astype(bf16)


def thirds(value):
    high = value.astype(bf16)
    rest = value - high.astype(f32)
    middle = rest.astype(bf16)
    return high, middle, (rest - middle.astype(f32)).astype(bf16)


def split_rows(cells):
    return [cells // 4] * 4


def column_mask(k_ref, group, spots):
    line = jnp.broadcast_to(k_ref[group : group + 1, :].astype(f32), (128, 128)).T
    return jnp.concatenate([line] * (spots // 128), axis=1)


def in_hbm(value):
    return pltpu.with_memory_space_constraint(value, pltpu.HBM)


def first_call(logits, keep_rows, size):
    spots = logits.shape[1]

    def body(x_ref, k_ref, o_ref, x_buf, sem):
        copy = pltpu.make_async_copy(x_ref.at[pl.ds(0, size)], x_buf, sem)
        copy.start()
        copy.wait()
        for g in range(size // 128):
            at = slice(g * 128, (g + 1) * 128)
            o_ref[at, :] = (jnp.exp(x_buf[at, :]) * column_mask(k_ref, g, spots)).astype(bf16)

    return pl.pallas_call(
        body,
        in_specs=[HBM, VMEM],
        out_specs=VMEM,
        out_shape=shape((size, spots), bf16),
        scratch_shapes=[pltpu.VMEM((size, spots), f32), pltpu.SemaphoreType.DMA],
        compiler_params=params(),
        cost_estimate=cost(0, 6 * size * spots),
        name="exp_first",
    )(in_hbm(logits), keep_rows)


def exp_call(logits, keep_rows, expression, ids, picks, sizes):
    cells, spots = logits.shape
    block = expression.shape[1] // ids.shape[0]
    tile = 512
    steps = cells // tile
    slots = min(4, steps)
    starts = [sum(sizes[:c]) for c in range(len(sizes))]
    count = len(picks)

    def body(ids_ref, x_ref, k_ref, e_ref, *refs):
        piece_refs = (None, *refs[: len(sizes) - 1])
        all_ref, s_ref, *refs = refs[len(sizes) - 1 :]
        o_refs, (u_buf, x_buf, held, sem, p_sem, a_sem, e_sem) = refs[:count], refs[count:]

        def fetch(t):
            return pltpu.make_async_copy(
                x_ref.at[pl.ds(t * tile, tile)], x_buf.at[t % slots], sem.at[t % slots]
            )

        for t in range(slots):
            fetch(t).start()
        copies = []
        for q, pick in enumerate(picks):
            at = pl.ds(pl.multiple_of(ids_ref[pick] * block, block), block)
            copies.append(pltpu.make_async_copy(e_ref.at[:, at], held.at[q], e_sem.at[q]))
            copies[q].start()
        total = jnp.zeros((8, spots), f32)
        sent = []
        for t in range(steps):
            fetch(t).wait()
            for g in range(tile // 128):
                at = slice(t * tile + g * 128, t * tile + (g + 1) * 128)
                rise = jnp.exp(x_buf[t % slots, g * 128 : (g + 1) * 128, :])
                rise = rise * column_mask(k_ref, t * (tile // 128) + g, spots)
                u_buf[at, :] = rise.astype(bf16)
                total = total + jnp.sum(rise.reshape(16, 8, spots), axis=0)
            if t + slots < steps:
                fetch(t + slots).start()
            for c in range(1, len(sizes)):
                if starts[c] + sizes[c] == (t + 1) * tile:
                    copy = pltpu.make_async_copy(
                        u_buf.at[pl.ds(starts[c], sizes[c])], piece_refs[c], p_sem.at[c]
                    )
                    copy.start()
                    sent.append(copy)
            if t % 2:
                at = pl.ds((t - 1) * tile, 2 * tile)
                copy = pltpu.make_async_copy(u_buf.at[at], all_ref.at[at], a_sem.at[t // 2])
                copy.start()
                sent.append(copy)
        kept = jnp.full((1, spots), jnp.sum(k_ref[...].astype(f32)), f32)
        total = jnp.sum(total, axis=0, keepdims=True)
        tops = jnp.concatenate([total, kept, jnp.zeros((6, spots), f32)], axis=0)
        s_ref[...] = tops
        for q in range(count):
            copies[q].wait()
            o_refs[q][0:block, :] = dot(held[q], u_buf[...], TN).astype(bf16)
            if q == 0:
                o_refs[0][block : block + 16, :] = packed(tops)
        for copy in sent:
            copy.wait()

    return pl.pallas_call(
        body,
        in_specs=[SMEM, HBM, VMEM, HBM],
        out_specs=[HBM] * len(sizes) + [VMEM] * (1 + count),
        out_shape=[pltpu.HBM((size, spots), bf16) for size in (*sizes[1:], cells)]
        + [shape((8, spots), f32)]
        + [shape((block + 16 * (q == 0), spots), bf16) for q in range(count)],
        scratch_shapes=[
            pltpu.VMEM((cells, spots), bf16),
            pltpu.VMEM((slots, tile, spots), f32),
            pltpu.VMEM((count, cells, block), bf16),
            pltpu.SemaphoreType.DMA((slots,)),
            pltpu.SemaphoreType.DMA((len(sizes),)),
            pltpu.SemaphoreType.DMA((steps // 2,)),
            pltpu.SemaphoreType.DMA((count,)),
        ],
        compiler_params=params(),
        cost_estimate=cost(0, 8 * cells * spots),
        name="exp_rows",
    )(ids, in_hbm(logits), keep_rows, in_hbm(expression))


def part_call(expression, mapping, ids, picks, dtypes):
    cells, spots = mapping.shape
    count = len(picks)
    block = expression.shape[1] // ids.shape[0]

    def body(ids_ref, e_ref, u_ref, *refs):
        o_refs, (held, sem) = refs[:count], refs[count:]
        copies = []
        for q, pick in enumerate(picks):
            at = pl.ds(pl.multiple_of(ids_ref[pick] * block, block), block)
            copies.append(pltpu.make_async_copy(e_ref.at[:, at], held.at[q], sem.at[q]))
            copies[q].start()
        for q in range(count):
            copies[q].wait()
            o_refs[q][...] = dot(held[q], u_ref[...], TN).astype(dtypes[q])

    return pl.pallas_call(
        body,
        in_specs=[SMEM, HBM, VMEM],
        out_specs=[VMEM] * count,
        out_shape=[shape((block, spots), dtype) for dtype in dtypes],
        scratch_shapes=[
            pltpu.VMEM((count, cells, block), bf16),
            pltpu.SemaphoreType.DMA((count,)),
        ],
        compiler_params=params(),
        cost_estimate=cost(
            2 * count * block * cells * spots, 2 * cells * (count * block + spots)
        ),
        name="part",
    )(ids, in_hbm(expression), mapping)


def add_call(values):
    def body(*refs):
        total = refs[0][...].astype(f32)
        for ref in refs[1:-1]:
            total = total + ref[...].astype(f32)
        refs[-1][...] = total.astype(bf16)

    return pl.pallas_call(
        body,
        out_shape=shape(values[0].shape, bf16),
        compiler_params=params(),
        cost_estimate=cost(0, 8 * values[0].size),
        name="add_blocks",
    )(*values)


def packed(tops):
    rows = jnp.concatenate([part.astype(f32) for part in thirds(tops[0:2, :])], axis=0)
    return jnp.concatenate([rows, jnp.zeros((10, tops.shape[1]), f32)], axis=0).astype(bf16)


def unpacked(rows):
    rows = rows.astype(f32)
    two = rows[0:2, :] + rows[2:4, :] + rows[4:6, :]
    return jnp.concatenate([two, jnp.zeros((6, rows.shape[1]), f32)], axis=0)


def relay_call(values, tops):
    block, spots = values[0].shape

    def body(*refs):
        *v_refs, tops_ref, o_ref, t_ref = refs
        total = v_refs[0][...].astype(f32)
        for ref in v_refs[1:]:
            total = total + ref[0:block, :].astype(f32)
        o_ref[0:block, :] = total.astype(bf16)
        tops_now = tops_ref[...] + unpacked(v_refs[-1][block : block + 16, :])
        t_ref[...] = tops_now
        o_ref[block : block + 16, :] = packed(tops_now)

    return pl.pallas_call(
        body,
        in_specs=[VMEM] * (len(values) + 1),
        out_specs=[VMEM] * 2,
        out_shape=[shape((block + 16, spots), bf16), shape(tops.shape, f32)],
        compiler_params=params(),
        cost_estimate=cost(0, 8 * block * spots),
        name="relay",
    )(*values, tops)


def total_of(tops_ref):
    return tops_ref[0:1, :]


def kept_of(tops_ref):
    return tops_ref[1:2, 0:1]


def predicted_call(values, tops, target, member):
    block, spots = target.shape
    slides = member.shape[0]
    more = values[-1].shape[0] > block

    def body(*refs):
        v_refs, (tops_ref, t_ref, m_ref, p_ref, near_ref, s_ref, all_ref) = refs[:-7], refs[-7:]
        total = v_refs[0][...].astype(f32)
        for ref in v_refs[1:]:
            total = total + ref[0:block, :].astype(f32)
        tops_now = tops_ref[...]
        if more:
            tops_now = tops_now + unpacked(v_refs[-1][block : block + 16, :])
        all_ref[...] = tops_now
        pred = total / tops_now[0:1, :]
        p_ref[...] = pred
        near_ref[...] = pred
        target_now = t_ref[...]
        member_low = m_ref[...].astype(bf16)
        for q, value in enumerate((pred * target_now, pred * pred, target_now * target_now)):
            high, low = halves(value)
            s_ref[q * slides : (q + 1) * slides, :] = dot(member_low, high, NT) + dot(
                member_low, low, NT
            )

    return pl.pallas_call(
        body,
        in_specs=[VMEM] * (len(values) + 3),
        out_specs=[VMEM] * 4,
        out_shape=[
            shape((block, spots), f32),
            shape((block, spots), f32),
            shape((3 * slides, block), f32),
            shape(tops.shape, f32),
        ],
        compiler_params=params(),
        cost_estimate=cost(0, 16 * block * spots),
        name="predicted",
    )(*values, tops, target, member)


def grad_call(sums, far, pred, target, tops, member):
    block, spots = target.shape
    slides = member.shape[0]

    def body(s_ref, f_ref, p_ref, t_ref, tops_ref, m_ref, g_ref, e_ref):
        total = s_ref[...] + f_ref[...]
        inner = total[0:slides, :]
        inv_predict = lax.rsqrt(total[slides : 2 * slides, :] + norm_eps)
        inv_target = lax.rsqrt(total[2 * slides : 3 * slides, :] + norm_eps)
        pair = inv_predict * inv_target
        cosine = inner * pair
        member_low = m_ref[...].astype(bf16)
        pair_at = sum(dot(v, member_low, TN) for v in thirds(pair))
        curve_at = sum(dot(v, member_low, TN) for v in thirds(cosine * inv_predict * inv_predict))
        pred = p_ref[...]
        grad = (pred * curve_at - t_ref[...] * pair_at) / total_of(tops_ref)
        grad = grad.astype(bf16)
        g_ref[...] = grad
        column = jnp.sum(pred * grad.astype(f32), axis=0, keepdims=True)
        total = jnp.sum(jnp.sum(cosine, axis=1, keepdims=True), axis=0, keepdims=True)
        e_ref[...] = jnp.concatenate(
            [column, jnp.broadcast_to(total, (1, spots)), jnp.zeros((6, spots), f32)], axis=0
        )

    return pl.pallas_call(
        body,
        out_shape=[shape((block, spots), bf16), shape((8, spots), f32)],
        compiler_params=params(),
        cost_estimate=cost(0, 12 * block * spots),
        name="grad",
    )(sums, far, pred, target, tops, member)


def density_call(mapping, tops, member):
    cells, spots = mapping.shape
    slides = member.shape[0]
    tile = min(cells, 1024)

    def body(u_ref, tops_ref, m_ref, o_ref):
        high, low = halves(m_ref[...] / total_of(tops_ref))
        pad = jnp.zeros((128 - 2 * slides, spots), bf16)
        both = jnp.concatenate([high, low, pad], axis=0)
        for t in range(cells // tile):
            at = slice(t * tile, (t + 1) * tile)
            got = dot(u_ref[at, :], both, NT).T
            o_ref[:, at] = got[0:slides, :] + got[slides : 2 * slides, :]

    return pl.pallas_call(
        body,
        in_specs=[VMEM] * 3,
        out_specs=VMEM,
        out_shape=shape((slides, cells), f32),
        compiler_params=params(),
        cost_estimate=cost(0, 2 * cells * spots),
        name="density",
    )(mapping, tops, member)


def diverge_call(density, far, keep_line, counts, mapping, tops, member):
    cells, spots = mapping.shape
    slides = member.shape[0]

    def body(d_ref, f_ref, k_ref, c_ref, u_ref, tops_ref, m_ref, o_ref, w_ref, e_ref):
        keep = k_ref[...].astype(f32)
        kept = kept_of(tops_ref)
        total = total_of(tops_ref)
        safe = jnp.where(keep > 0, d_ref[...] + f_ref[...], 1.0)
        high, low = halves(-density_weight * keep / (kept * safe))
        o_ref[...] = jnp.concatenate([high, high, low, jnp.zeros_like(low)], axis=0)
        w_high, w_low = halves(m_ref[...] / total)
        w_ref[...] = jnp.concatenate([w_high, w_low, w_high, jnp.zeros_like(w_low)], axis=0)
        column = jnp.zeros((8, spots), f32)
        chunk = 256
        for r in range(cells // chunk):
            at = slice(r * chunk, (r + 1) * chunk)
            pulled = dot(o_ref[:, at], w_ref[...], TN) * u_ref[at, :].astype(f32)
            column += jnp.sum(pulled.reshape(chunk // 8, 8, spots), axis=0)
        column = jnp.sum(column, axis=0, keepdims=True) / total
        logs = jnp.sum(jnp.log(safe), axis=0, keepdims=True)
        logs = -jnp.sum(logs, axis=1, keepdims=True)
        scale = jnp.sum(jnp.log(c_ref[...].astype(f32)), axis=1, keepdims=True)
        scale = scale - slides * jnp.log(kept)
        diverge = (logs + scale * jnp.sum(keep, axis=1, keepdims=True)) / kept
        e_ref[...] = jnp.concatenate(
            [
                column,
                jnp.zeros_like(column),
                jnp.broadcast_to(diverge, (1, spots)),
                jnp.zeros((5, spots), f32),
            ],
            axis=0,
        )

    return pl.pallas_call(
        body,
        in_specs=[VMEM] * 7,
        out_specs=[VMEM] * 3,
        out_shape=[
            shape((4 * slides, cells), bf16),
            shape((4 * slides, spots), bf16),
            shape((8, spots), f32),
        ],
        compiler_params=params(),
        cost_estimate=cost(0, 2 * cells * spots),
        name="diverge",
    )(density, far, keep_line, counts, mapping, tops, member)


def regroup_call(blocks, ids, place, spread):
    count = len(blocks)
    block, spots = blocks[0].shape
    share = count * block // spread

    def body(ids_ref, place_ref, *refs):
        b_refs, o_refs = refs[:count], refs[count : count + spread]
        held, in_sem, out_sem = refs[count + spread :]

        def rows(start, size):
            return held.at[pl.ds(pl.multiple_of(start, size), size)]

        copies = [
            pltpu.make_async_copy(b_refs[q], rows(ids_ref[q] * block, block), in_sem.at[q])
            for q in range(count)
        ]
        for copy in copies:
            copy.start()
        for copy in copies:
            copy.wait()
        copies = [
            pltpu.make_async_copy(rows((place_ref[0] ^ w) * share, share), o_refs[w], out_sem.at[w])
            for w in range(spread)
        ]
        for copy in copies:
            copy.start()
        for copy in copies:
            copy.wait()

    return pl.pallas_call(
        body,
        in_specs=[SMEM, SMEM] + [ANY] * count,
        out_specs=[HBM] * spread,
        out_shape=[shape((share, spots), bf16)] * spread,
        scratch_shapes=[
            pltpu.VMEM((count * block, spots), bf16),
            pltpu.SemaphoreType.DMA((count,)),
            pltpu.SemaphoreType.DMA((spread,)),
        ],
        compiler_params=params(),
        cost_estimate=cost(0, 4 * count * block * spots),
        name="regroup",
    )(ids, place, *blocks)


def logit_call(expression, blocks, ids, mapping, slope, weight, ends, tops):
    cells, genes = expression.shape
    block, spots = blocks[0].shape
    count = len(blocks)
    tile = min(cells, 1024)

    def body(ids_ref, e_ref, u_ref, d_ref, w_ref, ends_ref, tops_ref, *refs):
        b_refs, (o_ref, held, sem) = refs[:count], refs[count:]

        @pl.when(pl.program_id(0) == 0)
        def _():
            copies = []
            for q in range(count):
                at = pl.ds(pl.multiple_of(ids_ref[q] * block, block), block)
                copies.append(pltpu.make_async_copy(b_refs[q], held.at[at], sem.at[q]))
            for copy in copies:
                copy.start()
            for copy in copies:
                copy.wait()

        at = pl.ds(pl.multiple_of(pl.program_id(0) * tile, tile), tile)
        acc = dot(e_ref[at, :], held[...])
        acc += dot(d_ref[...], w_ref[...], TN) - ends_ref[0:1, :]
        o_ref[...] = u_ref[at, :].astype(f32) * (acc * kept_of(tops_ref))

    return pl.pallas_call(
        body,
        grid=(cells // tile,),
        in_specs=[SMEM, VMEM, VMEM, pl.BlockSpec((slope.shape[0], tile), lambda i: (0, i))]
        + [VMEM] * 3
        + [ANY] * count,
        out_specs=pl.BlockSpec((tile, spots), lambda i: (i, 0)),
        out_shape=shape((cells, spots), f32),
        scratch_shapes=[pltpu.VMEM((genes, spots), bf16), pltpu.SemaphoreType.DMA((count,))],
        compiler_params=params(),
        cost_estimate=cost(2 * cells * genes * spots, 2 * cells * genes + 6 * cells * spots),
        name="grad_logits",
    )(ids, expression, mapping, slope, weight, ends, tops, *blocks)


def expr_call(base, mapping, chunks, grads, tops, start):
    genes, spots = grads[0].shape
    cells = base.shape[0] if mapping is None else mapping.shape[0]
    own = 0 if mapping is None else 1
    count = len(chunks[0])
    tile = 512
    tiles = [(c, t) for c in range(len(chunks)) for t in range(chunks[c][0].shape[0] // tile)]
    slots = min(3, len(tiles))
    flat = [v for chunk in chunks for v in chunk]

    def body(*refs):
        q_refs, refs = refs[: len(flat)], refs[len(flat) :]
        g_refs, refs = refs[: len(grads)], refs[len(grads) :]
        tops_ref, whole_ref, o_ref, held, whole, out, in_sem, whole_sem, out_sem = refs
        scale = expression_scale * kept_of(tops_ref)

        def fetch(k):
            c, t = tiles[k]
            copies = [
                pltpu.make_async_copy(
                    q_refs[c * count + q].at[pl.ds(t * tile, tile)],
                    held.at[k % slots, q],
                    in_sem.at[k % slots, q],
                )
                for q in range(count)
            ]
            at = pl.ds(start + k * tile, tile)
            copies.append(
                pltpu.make_async_copy(
                    whole_ref.at[at], whole.at[k % slots], whole_sem.at[k % slots]
                )
            )
            return copies

        def store(k):
            return pltpu.make_async_copy(
                out.at[k % 2], o_ref.at[pl.ds(start + k * tile, tile)], out_sem.at[k % 2]
            )

        for k in range(slots):
            for copy in fetch(k):
                copy.start()
        for k in range(len(tiles)):
            for copy in fetch(k):
                copy.wait()
            total = dot(held[k % slots, 0], g_refs[own][...], NT)
            for q in range(1, count):
                total = total + dot(held[k % slots, q], g_refs[own + q][...], NT)
            if own:
                total = total + dot(whole[k % slots], g_refs[0][...], NT)
            total = total * scale
            if not own:
                total = total + whole[k % slots]
            if k >= 2:
                store(k - 2).wait()
            out[k % 2] = total
            store(k).start()
            if k + slots < len(tiles):
                for copy in fetch(k + slots):
                    copy.start()
        for k in range(max(len(tiles) - 2, 0), len(tiles)):
            store(k).wait()

    operands = [*flat, *grads, tops, in_hbm(mapping) if own else base]
    rows = len(tiles) * tile
    return pl.pallas_call(
        body,
        in_specs=[ANY] * len(flat) + [VMEM] * (len(grads) + 1) + [HBM],
        out_specs=HBM,
        out_shape=pltpu.HBM((cells, genes), f32),
        input_output_aliases={} if own else {len(operands) - 1: 0},
        scratch_shapes=[
            pltpu.VMEM((slots, count, tile, spots), bf16),
            pltpu.VMEM((slots, tile, spots if own else genes), bf16 if own else f32),
            pltpu.VMEM((2, tile, genes), f32),
            pltpu.SemaphoreType.DMA((slots, count)),
            pltpu.SemaphoreType.DMA((slots,)),
            pltpu.SemaphoreType.DMA((2,)),
        ],
        compiler_params=params(),
        cost_estimate=cost(
            2 * rows * spots * len(grads) * genes, 2 * rows * spots * len(grads) + 4 * rows * genes
        ),
        name="grad_expression",
    )(*operands)


def per_device(n, m, logits, expression, target, keep_mask, slide_ids, slide_counts):
    cells, spots = logits.shape
    genes = expression.shape[1]
    block = genes // n
    slide_total = slide_counts.shape[0]
    levels = n.bit_length() - 1
    lead = levels - 3
    orders = [[1 << k for k in range(levels)] for _ in range(2)]
    orders[1][0], orders[1][1] = 2, 1
    me = lax.axis_index("cell")
    place = lax.axis_index("spot")
    core = place & 1

    def across(value, k):
        pairs = [
            (i * m + j, (i ^ orders[j & 1][k]) * m + j) for i in range(n) for j in range(m)
        ]
        return lax.ppermute(value, ("cell", "spot"), pairs)

    def over_spot(value, mask):
        return lax.ppermute(value, "spot", [(j, j ^ mask) for j in range(m)])

    def over_cell(value, cell_mask, spot_mask):
        pairs = [
            (i * m + j, (i ^ cell_mask) * m + (j ^ spot_mask)) for i in range(n) for j in range(m)
        ]
        return lax.ppermute(value, ("cell", "spot"), pairs)

    def sum_cell(value):
        for k in range(levels):
            value = value + across(value, k)
        return value

    def sum_spot(value, aside):
        other = over_spot(value, 1)
        mask = 2
        while mask < m:
            value = value + other
            if aside:
                other = over_cell(over_cell(value, 1, 0), 1, mask)
            else:
                other = over_spot(value, mask)
            mask *= 2
        return value, other

    def tie(value, others):
        return lax.optimization_barrier((value, *others))[0]

    last_out = []

    def after(value, others=()):
        tied = lax.optimization_barrier((value, *last_out, *others))[0]
        last_out.clear()
        return tied

    def done(outs):
        last_out.append(outs[0] if isinstance(outs, (list, tuple)) else outs)
        return outs

    def place_of(code):
        value = me
        for k in range(levels):
            if code[k]:
                value = value ^ jnp.where(core == 1, orders[1][k], orders[0][k])
        return value

    def codes(prefix):
        out = [prefix]
        while len(out[0]) < levels:
            out = [c + (b,) for c in out for b in (1, 0)]
        return out

    ids = jnp.stack([place_of(c) for c in codes(())])
    order = {c[lead:]: q for q, c in enumerate(codes((0,) * lead))}
    slides = jnp.arange(slide_total, dtype=jnp.int32)
    member = (slide_ids[None, :] == slides[:, None]).astype(f32)

    keep_rows = keep_mask.reshape(cells // 128, 128)
    sizes = split_rows(cells)
    starts = [sum(sizes[:c]) for c in range(len(sizes))]
    pieces = [done(first_call(logits, keep_rows, sizes[0]))]
    picks = [order[1, 1, 1], order[1, 0, 1]] if not lead and block % 128 == 0 else []
    outs = exp_call(logits, after(keep_rows), expression, ids, picks, sizes)
    pieces += outs[: len(sizes) - 1]
    mapping, sums, *parts = outs[len(sizes) - 1 :]
    done(sums)
    gathered = {}

    def send(c, others=()):
        piece = tie(pieces[c], others)
        for mask in range(2, m, 2):
            gathered[c, mask] = over_spot(piece, mask)

    def spread(c):
        for mask in range(2, m, 2):
            gathered[c, mask + 1] = over_spot(gathered[c, mask], 1)

    def far(c):
        return [gathered[c, mask] for mask in range(2, m, 2)]

    def wide(c):
        return [gathered[c, mask + 1] for mask in range(2, m, 2)]

    send(0)

    part, got, step = {}, {}, {}
    if not picks:
        tops = sum_cell(sums)
        have = dot(expression, mapping, TN).reshape(n, block, spots)
        have = jnp.take(have, ids, axis=0)
        for k in range(lead):
            half = have.shape[0] // 2
            have = have[half:] + across(have[:half].astype(bf16), k).astype(f32)
        for code, q in order.items():
            part[code] = have[q]
        for a in (1, 0):
            for b in (1, 0):
                got[1, a, b] = across(part[1, a, b].astype(bf16), lead)
        for b in (1, 0):
            part[0, 1, b] = add_call([part[0, 1, b], got[1, 1, b]])
            step[0, 1, b] = across(part[0, 1, b], lead + 1)
        part[0, 0, 1] = add_call([part[0, 0, 1], got[1, 0, 1], step[0, 1, 1]])
        last = across(part[0, 0, 1], lead + 2)
        send(1)
        send(2)
        spread(0)
    else:
        part[1, 1, 1], part[1, 0, 1] = parts
        got[1, 1, 1], got[1, 0, 1] = across(parts[0], 0), across(parts[1], 0)

        def products(first, second, dtype, others):
            picks = [order[first], order[second]]
            here = after(ids, others)
            return done(part_call(expression, mapping, here, picks, [dtype] * 2))

        part[0, 1, 1], part[0, 0, 1] = products((0, 1, 1), (0, 0, 1), f32, [])
        part[0, 1, 1], tops = done(
            relay_call([after(part[0, 1, 1], far(0)), got[1, 1, 1]], sums)
        )
        send(1, [part[0, 1, 1]])
        spread(0)
        step[0, 1, 1] = across(part[0, 1, 1], 1)
        part[1, 1, 0], part[1, 0, 0] = products((1, 1, 0), (1, 0, 0), bf16, [])
        got[1, 1, 0], got[1, 0, 0] = across(part[1, 1, 0], 0), across(part[1, 0, 0], 0)
        part[0, 0, 1], tops = done(
            relay_call([after(part[0, 0, 1]), got[1, 0, 1], step[0, 1, 1]], tops)
        )
        last = across(part[0, 0, 1], 2)
        part[0, 1, 0], part[0, 0, 0] = products((0, 1, 0), (0, 0, 0), f32, [])
        part[0, 1, 0] = done(add_call([after(part[0, 1, 0]), got[1, 1, 0]]))
        step[0, 1, 0] = across(part[0, 1, 0], 1)
        send(2, [part[0, 1, 0]])
    predicted, predicted_near, gene_sums, tops = done(
        predicted_call(
            [part[0, 0, 0], got[1, 0, 0], step[0, 1, 0], last],
            tops,
            target,
            after(member, far(1) + wide(0)),
        )
    )
    gene_sums, far_sums = sum_spot(gene_sums, True)
    density = done(density_call(mapping, tops, after(member)))
    density, far_density = sum_spot(density, True)
    beside = over_spot(tie(mapping, [density]), 1)
    grad, ends = done(
        grad_call(gene_sums, far_sums, predicted_near, target, tops, after(member))
    )
    send(3, [grad])

    have = {(0, 0, 0): grad}
    for k in (2, 1, 0):
        for code in list(have):
            other = tuple(1 if q == k else b for q, b in enumerate(code))
            have[other] = across(have[code], lead + k)
    tail = codes((0,) * lead)
    blocks = [have[c[lead:]] for c in tail]
    if lead:
        blocks = jnp.stack(blocks)
        for k in reversed(range(lead)):
            blocks = jnp.concatenate([across(blocks, k), blocks])
        blocks = [blocks[q] for q in range(n)]

    slope, weight, more = done(
        diverge_call(
            density,
            far_density,
            keep_mask[None, :],
            slide_counts[None, :],
            mapping,
            tops,
            after(member, [have[0, 1, 0], beside]),
        )
    )
    ends = sum_cell(ends + more)
    mapping_loss = (-ends[1, 0] + density_weight * ends[2, 0]) / (slide_total * genes)

    spread(1)
    shares = done(regroup_call(blocks, after(ids, far(2)), place[None], m))
    spread(2)
    regrouped = [None] * m
    for mask in range(0, m, 2):
        regrouped[mask] = over_spot(shares[mask], mask) if mask else shares[0]
        other = over_spot(shares[mask + 1], mask) if mask else shares[1]
        regrouped[mask + 1] = over_spot(other, 1)

    grad_logits = done(
        logit_call(
            expression,
            blocks,
            ids,
            mapping,
            slope,
            weight,
            after(ends, [*wide(1), *wide(2), regrouped[1]]),
            tops,
        )
    )
    near_part = done(
        expr_call(None, mapping, [[beside]], regrouped[:2], after(tops, far(3)), 0)
    )
    spread(3)
    rest = [[gathered[c, mask] for mask in range(2, m)] for c in range(4)]
    grad_expression = expr_call(near_part, None, rest, regrouped[2:], after(tops), 0)
    return (mapping_loss, predicted, grad_logits, grad_expression)


def solution(mesh):
    in_specs = (P("cell", "spot"), P("cell", None), P("cell", "spot"), P("cell"), P("spot"), P())
    out_specs = (P(), P("cell", "spot"), P("cell", "spot"), P("cell", "spot"))
    body = functools.partial(per_device, mesh.shape["cell"], mesh.shape["spot"])
    return jax.shard_map(
        body, mesh=mesh, in_specs=in_specs, out_specs=out_specs, check_vma=False
    )
```

```python
import functools

import jax
import jax.numpy as jnp
from jax import lax
from jax.experimental import pallas as pl
from jax.experimental.pallas import tpu as pltpu
from jax.sharding import PartitionSpec as P

density_weight = 32.0
expression_scale = 64.0
norm_eps = 1e-06
f32 = jnp.float32
bf16 = jnp.bfloat16
VMEM_LIMIT = 20 << 20
COST_SHARE = 0.05
NT = (((1,), (1,)), ((), ()))
TN = (((0,), (0,)), ((), ()))


def cost(flops, bytes_accessed, share=COST_SHARE):
    return pl.CostEstimate(
        flops=int(flops * share),
        bytes_accessed=int(bytes_accessed * share),
        transcendentals=0,
    )


ANY = pl.BlockSpec(memory_space=pl.ANY)
HBM = pl.BlockSpec(memory_space=pltpu.HBM)
VMEM = pl.BlockSpec(memory_space=pltpu.VMEM)
SMEM = pl.BlockSpec(memory_space=pltpu.SMEM)


def params():
    return pltpu.CompilerParams(vmem_limit_bytes=VMEM_LIMIT)


def shape(dims, dtype):
    return jax.ShapeDtypeStruct(dims, dtype)


def dot(a, b, dims=(((1,), (0,)), ((), ()))):
    return lax.dot_general(a, b, dims, preferred_element_type=f32)


def halves(value):
    high = value.astype(bf16)
    return high, (value - high.astype(f32)).astype(bf16)


def thirds(value):
    high = value.astype(bf16)
    rest = value - high.astype(f32)
    middle = rest.astype(bf16)
    return high, middle, (rest - middle.astype(f32)).astype(bf16)


def split_rows(cells):
    unit = cells // 64
    return [share * unit for share in (16, 20, 24, 4)]


def column_mask(k_ref, group, spots):
    line = jnp.broadcast_to(k_ref[group : group + 1, :].astype(f32), (128, 128)).T
    return jnp.concatenate([line] * (spots // 128), axis=1)


def in_hbm(value):
    return pltpu.with_memory_space_constraint(value, pltpu.HBM)


def first_call(logits, keep_rows, size):
    spots = logits.shape[1]

    def body(x_ref, k_ref, o_ref, x_buf, k_buf, sem):
        copies = [pltpu.make_async_copy(k_ref, k_buf, sem.at[0])]
        for g in range(size // 128):
            at = pl.ds(g * 128, 128)
            copies.append(pltpu.make_async_copy(x_ref.at[at], x_buf.at[at], sem.at[g + 1]))
        for copy in copies:
            copy.start()
        copies[0].wait()
        for g in range(size // 128):
            at = slice(g * 128, (g + 1) * 128)
            copies[g + 1].wait()
            o_ref[at, :] = (jnp.exp(x_buf[at, :]) * column_mask(k_buf, g, spots)).astype(bf16)

    return pl.pallas_call(
        body,
        in_specs=[HBM, HBM],
        out_specs=VMEM,
        out_shape=shape((size, spots), bf16),
        scratch_shapes=[
            pltpu.VMEM((size, spots), f32),
            pltpu.VMEM(keep_rows.shape, jnp.int32),
            pltpu.SemaphoreType.DMA((size // 128 + 1,)),
        ],
        compiler_params=params(),
        cost_estimate=cost(0, 6 * size * spots),
        name="exp_first",
    )(in_hbm(logits), in_hbm(keep_rows))


def exp_call(logits, keep_rows, expression, ids, picks, sizes):
    cells, spots = logits.shape
    block = expression.shape[1] // ids.shape[0]
    tile = 512
    steps = cells // tile
    slots = min(3, steps)
    starts = [sum(sizes[:c]) for c in range(len(sizes))]
    count = len(picks)

    def body(ids_ref, x_ref, k_ref, e_ref, *refs):
        piece_refs = (None, *refs[: len(sizes) - 1])
        all_ref, s_ref, *refs = refs[len(sizes) - 1 :]
        o_refs, refs = refs[:count], refs[count:]
        u_buf, x_buf, held, acc, k_buf, sem, p_sem, a_sem, e_sem, k_sem = refs
        keep = pltpu.make_async_copy(k_ref, k_buf, k_sem)
        keep.start()

        def fetch(t):
            return pltpu.make_async_copy(
                x_ref.at[pl.ds(t * tile, tile)], x_buf.at[t % slots], sem.at[t % slots]
            )

        for t in range(slots):
            fetch(t).start()
        half = cells // 2

        def hold(h, q):
            at = pl.ds(pl.multiple_of(ids_ref[picks[q]] * block, block), block)
            rows = pl.ds(h * half, half)
            return pltpu.make_async_copy(e_ref.at[rows, at], held.at[q], e_sem.at[q])

        for q in range(count):
            hold(0, q).start()
        total = jnp.zeros((8, spots), f32)
        sent = []
        keep.wait()
        for t in range(steps):
            fetch(t).wait()
            for g in range(tile // 128):
                at = slice(t * tile + g * 128, t * tile + (g + 1) * 128)
                rise = jnp.exp(x_buf[t % slots, g * 128 : (g + 1) * 128, :])
                rise = rise * column_mask(k_buf, t * (tile // 128) + g, spots)
                u_buf[at, :] = rise.astype(bf16)
                total = total + jnp.sum(rise.reshape(16, 8, spots), axis=0)
            if t + slots < steps:
                fetch(t + slots).start()
            for c in range(1, len(sizes)):
                if t * tile < starts[c] + sizes[c] <= (t + 1) * tile:
                    copy = pltpu.make_async_copy(
                        u_buf.at[pl.ds(starts[c], sizes[c])], piece_refs[c], p_sem.at[c]
                    )
                    copy.start()
                    sent.append(copy)
            if t % 2:
                at = pl.ds((t - 1) * tile, 2 * tile)
                copy = pltpu.make_async_copy(u_buf.at[at], all_ref.at[at], a_sem.at[t // 2])
                copy.start()
                sent.append(copy)
            if t == steps // 2 - 1:
                for q in range(count):
                    hold(0, q).wait()
                    acc[q] = dot(held[q], u_buf[0:half, :], TN)
                    hold(1, q).start()
        kept = jnp.full((1, spots), jnp.sum(k_buf[...].astype(f32)), f32)
        total = jnp.sum(total, axis=0, keepdims=True)
        tops = jnp.concatenate([total, kept, jnp.zeros((6, spots), f32)], axis=0)
        s_ref[...] = tops
        for q in range(count):
            hold(1, q).wait()
            term = dot(held[q], u_buf[half:cells, :], TN)
            o_refs[q][0:block, :] = (acc[q] + term).astype(bf16)
            if q == 0:
                o_refs[0][block : block + 16, :] = packed(tops)
        for copy in sent:
            copy.wait()

    return pl.pallas_call(
        body,
        in_specs=[SMEM, HBM, HBM, HBM],
        out_specs=[HBM] * len(sizes) + [VMEM] * (1 + count),
        out_shape=[pltpu.HBM((size, spots), bf16) for size in (*sizes[1:], cells)]
        + [shape((8, spots), f32)]
        + [shape((block + 16 * (q == 0), spots), bf16) for q in range(count)],
        scratch_shapes=[
            pltpu.VMEM((cells, spots), bf16),
            pltpu.VMEM((slots, tile, spots), f32),
            pltpu.VMEM((count, cells // 2, block), bf16),
            pltpu.VMEM((count, block, spots), f32),
            pltpu.VMEM(keep_rows.shape, jnp.int32),
            pltpu.SemaphoreType.DMA((slots,)),
            pltpu.SemaphoreType.DMA((len(sizes),)),
            pltpu.SemaphoreType.DMA((steps // 2,)),
            pltpu.SemaphoreType.DMA((count,)),
            pltpu.SemaphoreType.DMA,
        ],
        compiler_params=params(),
        cost_estimate=cost(0, 8 * cells * spots),
        name="exp_rows",
    )(ids, in_hbm(logits), in_hbm(keep_rows), in_hbm(expression))


def part_call(expression, mapping, ids, picks, dtypes):
    cells, spots = mapping.shape
    count = len(picks)
    block = expression.shape[1] // ids.shape[0]

    def body(ids_ref, e_ref, u_ref, *refs):
        o_refs, (held, sem) = refs[:count], refs[count:]
        copies = []
        for q, pick in enumerate(picks):
            at = pl.ds(pl.multiple_of(ids_ref[pick] * block, block), block)
            copies.append(pltpu.make_async_copy(e_ref.at[:, at], held.at[q], sem.at[q]))
            copies[q].start()
        for q in range(count):
            copies[q].wait()
            o_refs[q][...] = dot(held[q], u_ref[...], TN).astype(dtypes[q])

    return pl.pallas_call(
        body,
        in_specs=[SMEM, HBM, VMEM],
        out_specs=[VMEM] * count,
        out_shape=[shape((block, spots), dtype) for dtype in dtypes],
        scratch_shapes=[
            pltpu.VMEM((count, cells, block), bf16),
            pltpu.SemaphoreType.DMA((count,)),
        ],
        compiler_params=params(),
        cost_estimate=cost(
            2 * count * block * cells * spots, 2 * cells * (count * block + spots)
        ),
        name="part",
    )(ids, in_hbm(expression), mapping)


def add_call(values):
    def body(*refs):
        total = refs[0][...].astype(f32)
        for ref in refs[1:-1]:
            total = total + ref[...].astype(f32)
        refs[-1][...] = total.astype(bf16)

    return pl.pallas_call(
        body,
        out_shape=shape(values[0].shape, bf16),
        compiler_params=params(),
        cost_estimate=cost(0, 8 * values[0].size),
        name="add_blocks",
    )(*values)


def packed(tops):
    rows = jnp.concatenate([part.astype(f32) for part in thirds(tops[0:2, :])], axis=0)
    return jnp.concatenate([rows, jnp.zeros((10, tops.shape[1]), f32)], axis=0).astype(bf16)


def unpacked(rows):
    rows = rows.astype(f32)
    two = rows[0:2, :] + rows[2:4, :] + rows[4:6, :]
    return jnp.concatenate([two, jnp.zeros((6, rows.shape[1]), f32)], axis=0)


def relay_call(values, tops):
    block, spots = values[0].shape

    def body(*refs):
        *v_refs, tops_ref, o_ref, t_ref = refs
        total = v_refs[0][...].astype(f32)
        for ref in v_refs[1:]:
            total = total + ref[0:block, :].astype(f32)
        o_ref[0:block, :] = total.astype(bf16)
        tops_now = tops_ref[...] + unpacked(v_refs[-1][block : block + 16, :])
        t_ref[...] = tops_now
        o_ref[block : block + 16, :] = packed(tops_now)

    return pl.pallas_call(
        body,
        in_specs=[VMEM] * (len(values) + 1),
        out_specs=[VMEM] * 2,
        out_shape=[shape((block + 16, spots), bf16), shape(tops.shape, f32)],
        compiler_params=params(),
        cost_estimate=cost(0, 8 * block * spots),
        name="relay",
    )(*values, tops)


def hold_call(value, others):
    def body(*refs):
        refs[-1][...] = refs[-2][...]

    return pl.pallas_call(
        body,
        in_specs=[VMEM] * (1 + len(others)),
        out_specs=VMEM,
        out_shape=shape(value.shape, value.dtype),
        compiler_params=params(),
        cost_estimate=cost(0, 0),
        name="hold",
    )(*others, value)


def total_of(tops_ref):
    return tops_ref[0:1, :]


def kept_of(tops_ref):
    return tops_ref[1:2, 0:1]


def predicted_call(values, tops, target, member):
    block, spots = target.shape
    slides = member.shape[0]
    more = values[-1].shape[0] > block

    def body(*refs):
        v_refs, (tops_ref, t_ref, m_ref, p_ref, near_ref, s_ref, all_ref) = refs[:-7], refs[-7:]
        total = v_refs[0][...].astype(f32)
        for ref in v_refs[1:]:
            total = total + ref[0:block, :].astype(f32)
        tops_now = tops_ref[...]
        if more:
            tops_now = tops_now + unpacked(v_refs[-1][block : block + 16, :])
        all_ref[...] = tops_now
        pred = total / tops_now[0:1, :]
        p_ref[...] = pred
        near_ref[...] = pred
        target_now = t_ref[...]
        member_low = m_ref[...].astype(bf16)
        for q, value in enumerate((pred * target_now, pred * pred, target_now * target_now)):
            high, low = halves(value)
            s_ref[q * slides : (q + 1) * slides, :] = dot(member_low, high, NT) + dot(
                member_low, low, NT
            )

    return pl.pallas_call(
        body,
        in_specs=[VMEM] * (len(values) + 3),
        out_specs=[VMEM] * 4,
        out_shape=[
            shape((block, spots), f32),
            shape((block, spots), f32),
            shape((3 * slides, block), f32),
            shape(tops.shape, f32),
        ],
        compiler_params=params(),
        cost_estimate=cost(0, 16 * block * spots),
        name="predicted",
    )(*values, tops, target, member)


def grad_call(sums, far, pred, target, tops, member):
    block, spots = target.shape
    slides = member.shape[0]

    def body(s_ref, f_ref, p_ref, t_ref, tops_ref, m_ref, g_ref, e_ref):
        total = s_ref[...] + f_ref[...]
        inner = total[0:slides, :]
        inv_predict = lax.rsqrt(total[slides : 2 * slides, :] + norm_eps)
        inv_target = lax.rsqrt(total[2 * slides : 3 * slides, :] + norm_eps)
        pair = inv_predict * inv_target
        cosine = inner * pair
        member_low = m_ref[...].astype(bf16)
        pair_at = sum(dot(v, member_low, TN) for v in thirds(pair))
        curve_at = sum(dot(v, member_low, TN) for v in thirds(cosine * inv_predict * inv_predict))
        pred = p_ref[...]
        grad = (pred * curve_at - t_ref[...] * pair_at) / total_of(tops_ref)
        grad = grad.astype(bf16)
        g_ref[...] = grad
        column = jnp.sum(pred * grad.astype(f32), axis=0, keepdims=True)
        total = jnp.sum(jnp.sum(cosine, axis=1, keepdims=True), axis=0, keepdims=True)
        e_ref[...] = jnp.concatenate(
            [column, jnp.broadcast_to(total, (1, spots)), jnp.zeros((6, spots), f32)], axis=0
        )

    return pl.pallas_call(
        body,
        out_shape=[shape((block, spots), bf16), shape((8, spots), f32)],
        compiler_params=params(),
        cost_estimate=cost(0, 12 * block * spots),
        name="grad",
    )(sums, far, pred, target, tops, member)


def density_call(mapping, tops, member):
    cells, spots = mapping.shape
    slides = member.shape[0]
    tile = min(cells, 1024)

    def body(u_ref, tops_ref, m_ref, o_ref):
        high, low = halves(m_ref[...] / total_of(tops_ref))
        pad = jnp.zeros((128 - 2 * slides, spots), bf16)
        both = jnp.concatenate([high, low, pad], axis=0)
        for t in range(cells // tile):
            at = slice(t * tile, (t + 1) * tile)
            got = dot(u_ref[at, :], both, NT).T
            o_ref[:, at] = got[0:slides, :] + got[slides : 2 * slides, :]

    return pl.pallas_call(
        body,
        in_specs=[VMEM] * 3,
        out_specs=VMEM,
        out_shape=shape((slides, cells), f32),
        compiler_params=params(),
        cost_estimate=cost(0, 2 * cells * spots),
        name="density",
    )(mapping, tops, member)


def diverge_call(density, far, keep_line, counts, mapping, tops, member):
    cells, spots = mapping.shape
    slides = member.shape[0]

    def body(d_ref, f_ref, k_ref, c_ref, u_ref, tops_ref, m_ref, s_ref, w_ref, e_ref, o_ref, sem):
        keep = k_ref[...].astype(f32)
        kept = kept_of(tops_ref)
        total = total_of(tops_ref)
        safe = jnp.where(keep > 0, d_ref[...] + f_ref[...], 1.0)
        high, low = halves(-density_weight * keep / (kept * safe))
        rest = jnp.concatenate([jnp.ones((8, cells), f32), jnp.zeros((96, cells), f32)], axis=0)
        parts = [high.astype(f32), high.astype(f32), low.astype(f32), rest]
        parts = jnp.concatenate(parts, axis=0)
        w_high, w_low = halves(m_ref[...] / total)
        w_ref[...] = jnp.concatenate([w_high, w_low, w_high, jnp.zeros_like(w_low)], axis=0)
        column = jnp.zeros((8, spots), f32)
        chunk = 256
        for r in range(cells // chunk):
            at = slice(r * chunk, (r + 1) * chunk)
            o_ref[at, :] = parts[:, at].T.astype(bf16)
            pulled = dot(o_ref[at, 0:32], w_ref[...]) * u_ref[at, :].astype(f32)
            column += jnp.sum(pulled.reshape(chunk // 8, 8, spots), axis=0)
        store = pltpu.make_async_copy(o_ref, s_ref, sem)
        store.start()
        column = jnp.sum(column, axis=0, keepdims=True) / total
        logs = jnp.sum(jnp.log(safe), axis=0, keepdims=True)
        logs = -jnp.sum(logs, axis=1, keepdims=True)
        scale = jnp.sum(jnp.log(c_ref[...].astype(f32)), axis=1, keepdims=True)
        scale = scale - slides * jnp.log(kept)
        diverge = (logs + scale * jnp.sum(keep, axis=1, keepdims=True)) / kept
        e_ref[...] = jnp.concatenate(
            [
                column,
                jnp.zeros_like(column),
                jnp.broadcast_to(diverge, (1, spots)),
                jnp.zeros((5, spots), f32),
            ],
            axis=0,
        )
        store.wait()

    return pl.pallas_call(
        body,
        in_specs=[VMEM] * 7,
        out_specs=[HBM, VMEM, VMEM],
        out_shape=[
            pltpu.HBM((cells, 128), bf16),
            shape((4 * slides, spots), bf16),
            shape((8, spots), f32),
        ],
        scratch_shapes=[pltpu.VMEM((cells, 128), bf16), pltpu.SemaphoreType.DMA],
        compiler_params=params(),
        cost_estimate=cost(0, 2 * cells * spots),
        name="diverge",
    )(density, far, keep_line, counts, mapping, tops, member)


def regroup_call(blocks, ids, place, spread):
    count = len(blocks)
    block, spots = blocks[0].shape
    share = count * block // spread

    def body(ids_ref, place_ref, *refs):
        b_refs, all_ref, o_refs = refs[:count], refs[count], refs[count + 1 : count + 1 + spread]
        in_sem, out_sem = refs[count + 1 + spread :]

        def rows(start, size):
            return all_ref.at[pl.ds(pl.multiple_of(start, size), size)]

        copies = [
            pltpu.make_async_copy(b_refs[q], rows(ids_ref[q] * block, block), in_sem.at[q])
            for q in range(count)
        ]
        for copy in copies:
            copy.start()
        for copy in copies:
            copy.wait()
        copies = [
            pltpu.make_async_copy(rows((place_ref[0] ^ w) * share, share), o_refs[w], out_sem.at[w])
            for w in range(spread)
        ]
        for copy in copies:
            copy.start()
        for copy in copies:
            copy.wait()

    return pl.pallas_call(
        body,
        in_specs=[SMEM, SMEM] + [ANY] * count,
        out_specs=[VMEM] + [HBM] * spread,
        out_shape=[shape((count * block, spots), bf16)]
        + [shape((share, spots), bf16)] * spread,
        scratch_shapes=[
            pltpu.SemaphoreType.DMA((count,)),
            pltpu.SemaphoreType.DMA((spread,)),
        ],
        compiler_params=params(),
        cost_estimate=cost(0, 4 * count * block * spots),
        name="regroup",
    )(ids, place, blocks[0], *[in_hbm(value) for value in blocks[1:]])


def logit_call(expression, grad, mapping, slope, weight, ends, tops, slides):
    cells, genes = expression.shape
    spots = grad.shape[1]
    tile = min(cells, 512)
    slots = 3
    runs = [(row, tile) for row in range(0, cells, tile)]

    def body(e_ref, g_ref, u_ref, d_ref, w_ref, ends_ref, tops_ref, *refs):
        o_ref, l_ref, held, e_buf, u_buf, out, in_sem, out_sem = refs

        def fetch(k):
            row, size = runs[k]
            copies = []
            to = (k % slots, pl.ds(0, size))
            copies.append(
                pltpu.make_async_copy(
                    e_ref.at[pl.ds(row, size)], e_buf.at[*to, pl.ds(0, genes)], in_sem.at[k % slots, 0]
                )
            )
            copies.append(
                pltpu.make_async_copy(
                    u_ref.at[pl.ds(row, size)], u_buf.at[*to], in_sem.at[k % slots, 1]
                )
            )
            copies.append(
                pltpu.make_async_copy(
                    d_ref.at[pl.ds(row, size)],
                    e_buf.at[*to, pl.ds(genes, 128)],
                    in_sem.at[k % slots, 2],
                )
            )
            return copies

        def store(k):
            row, size = runs[k]
            return pltpu.make_async_copy(
                out.at[k % 2, pl.ds(0, size)], o_ref.at[pl.ds(row, size)], out_sem.at[k % 2]
            )

        for copy in fetch(0):
            copy.start()
        held[0:genes, :] = g_ref[...]
        sums = jnp.concatenate([part.astype(f32) for part in thirds(-ends_ref[0:1, :])], axis=0)
        sums = jnp.concatenate([sums, jnp.zeros((101, spots), f32)], axis=0)
        weights = jnp.concatenate([w_ref[0:24, :].astype(f32), sums], axis=0)
        held[genes : genes + 128, :] = weights.astype(bf16)
        kept = kept_of(tops_ref)
        total = density_weight * ends_ref[2:3, 0:1] - ends_ref[1:2, 0:1]
        l_ref[...] = total / (genes * slides)
        following = 1
        for k, (row, size) in enumerate(runs):
            for copy in fetch(k):
                copy.wait()
            while following < min(k + slots, len(runs)):
                for copy in fetch(following):
                    copy.start()
                following += 1
            if k >= 2:
                store(k - 2).wait()
            acc = dot(e_buf[k % slots, 0:size], held[...])
            out[k % 2, 0:size] = (u_buf[k % slots, 0:size].astype(f32) * kept) * acc
            store(k).start()
        for k in range(len(runs) - 2, len(runs)):
            store(k).wait()

    return pl.pallas_call(
        body,
        in_specs=[HBM, VMEM, HBM, HBM] + [VMEM] * 3,
        out_specs=[HBM, VMEM],
        out_shape=[pltpu.HBM((cells, spots), f32), shape((1, 1), f32)],
        scratch_shapes=[
            pltpu.VMEM((genes + 128, spots), bf16),
            pltpu.VMEM((slots, tile, genes + 128), bf16),
            pltpu.VMEM((slots, tile, spots), bf16),
            pltpu.VMEM((2, tile, spots), f32),
            pltpu.SemaphoreType.DMA((slots, 3)),
            pltpu.SemaphoreType.DMA((2,)),
        ],
        compiler_params=params(),
        cost_estimate=cost(
            2 * cells * genes * spots, 2 * cells * genes + 6 * cells * spots, 0.0
        ),
        name="grad_logits",
    )(in_hbm(expression), grad, in_hbm(mapping), in_hbm(slope), weight, ends, tops)


def expr_call(base, mapping, chunks, grads, tops):
    genes, spots = grads[0].shape
    cells = mapping.shape[0] if base is None else base.shape[0]
    count = len(grads)
    tile = 512
    own = 0 if mapping is None else 1
    tiles, c, row = [], 0, 0
    for t in range(cells // tile):
        runs, filled = [], 0
        while filled < tile:
            size = min(tile - filled, chunks[c][0].shape[0] - row)
            runs.append((c, row, filled, size))
            filled, row = filled + size, row + size
            if row == chunks[c][0].shape[0]:
                c, row = c + 1, 0
        tiles.append(runs)
    most = max(len(runs) for runs in tiles)
    slots = 3
    flat = [v for chunk in chunks for v in chunk]
    far = count - own

    def body(*refs):
        q_refs, refs = refs[: len(flat)], refs[len(flat) :]
        g_refs, refs = refs[:count], refs[count:]
        tops_ref, whole_ref, o_ref, held, g_buf, out, in_sem, out_sem = refs
        scale = expression_scale * kept_of(tops_ref)

        def fetch(k):
            pieces = [
                (own + q, q_refs[c * far + q].at[pl.ds(row, size)], at, size, r)
                for r, (c, row, at, size) in enumerate(tiles[k])
                for q in range(far)
            ]
            if own:
                pieces.append((0, whole_ref.at[pl.ds(k * tile, tile)], 0, tile, 0))
            return [
                pltpu.make_async_copy(
                    source,
                    held.at[k % slots, pl.ds(at, size), pl.ds(q * spots, spots)],
                    in_sem.at[k % slots, q, r],
                )
                for q, source, at, size, r in pieces
            ]

        def store(k):
            return pltpu.make_async_copy(
                out.at[k % 2], o_ref.at[pl.ds(k * tile, tile)], out_sem.at[k % 2]
            )

        for k in range(slots):
            for copy in fetch(k):
                copy.start()
        for q in range(count):
            g_buf[:, q * spots : (q + 1) * spots] = g_refs[q][...]
        for k in range(len(tiles)):
            for copy in fetch(k):
                copy.wait()
            at = slice(k * tile, (k + 1) * tile)
            if own:
                o_ref[at, :] = dot(held[k % slots], g_buf[...], NT) * scale
            else:
                if k >= 2:
                    store(k - 2).wait()
                out[k % 2] = dot(held[k % slots], g_buf[...], NT) * scale + whole_ref[at, :]
                store(k).start()
            if k + slots < len(tiles):
                for copy in fetch(k + slots):
                    copy.start()
        if not own:
            for k in range(len(tiles) - 2, len(tiles)):
                store(k).wait()

    rows = len(tiles) * tile
    return pl.pallas_call(
        body,
        in_specs=[ANY] * len(flat) + [VMEM] * (count + 1) + [HBM if own else VMEM],
        out_specs=VMEM if own else HBM,
        out_shape=shape((cells, genes), f32) if own else pltpu.HBM((cells, genes), f32),
        scratch_shapes=[
            pltpu.VMEM((slots, tile, count * spots), bf16),
            pltpu.VMEM((genes, count * spots), bf16),
            pltpu.VMEM((2, tile, genes), f32),
            pltpu.SemaphoreType.DMA((slots, count, most)),
            pltpu.SemaphoreType.DMA((2,)),
        ],
        compiler_params=params(),
        cost_estimate=cost(
            2 * rows * spots * count * genes, 2 * rows * spots * count + 4 * rows * genes, 0.0
        ),
        name="grad_expression",
    )(*flat, *grads, tops, in_hbm(mapping) if own else base)


def per_device(n, m, logits, expression, target, keep_mask, slide_ids, slide_counts):
    cells, spots = logits.shape
    genes = expression.shape[1]
    block = genes // n
    slide_total = slide_counts.shape[0]
    levels = n.bit_length() - 1
    lead = levels - 3
    orders = [[1 << k for k in range(levels)] for _ in range(2)]
    orders[1][0], orders[1][1] = 2, 1
    me = lax.axis_index("cell")
    place = lax.axis_index("spot")
    core = place & 1

    def across(value, *levels_of):
        masks = [sum(order[k] for k in levels_of) for order in orders]
        pairs = [(i * m + j, (i ^ masks[j & 1]) * m + j) for i in range(n) for j in range(m)]
        return lax.ppermute(value, ("cell", "spot"), pairs)

    def over_spot(value, mask):
        return lax.ppermute(value, "spot", [(j, j ^ mask) for j in range(m)])

    def over_cell(value, cell_mask, spot_mask):
        pairs = [
            (i * m + j, (i ^ cell_mask) * m + (j ^ spot_mask)) for i in range(n) for j in range(m)
        ]
        return lax.ppermute(value, ("cell", "spot"), pairs)

    def sum_cell(value):
        for k in range(levels):
            value = value + across(value, k)
        return value

    def sum_spot(value):
        first = aside = other = over_spot(value, 1)
        mask = 2
        while mask < m:
            value = value + other
            first = value if mask == 2 else first
            aside = over_cell(value, 1, 0)
            other = over_cell(aside, 1, mask)
            mask *= 2
        return first, value, aside, other

    def tie(value, others):
        return lax.optimization_barrier((value, *others))[0]

    def corner(value):
        return value[:8, :128]

    last_out = []

    def after(value, others=()):
        tied = lax.optimization_barrier((value, *last_out, *others))[0]
        last_out.clear()
        return tied

    def done(outs):
        last_out.append(outs[0] if isinstance(outs, (list, tuple)) else outs)
        return outs

    def place_of(code):
        value = me
        for k in range(levels):
            if code[k]:
                value = value ^ jnp.where(core == 1, orders[1][k], orders[0][k])
        return value

    def codes(prefix):
        out = [prefix]
        while len(out[0]) < levels:
            out = [c + (b,) for c in out for b in (1, 0)]
        return out

    ids = jnp.stack([place_of(c) for c in codes(())])
    order = {c[lead:]: q for q, c in enumerate(codes((0,) * lead))}
    slides = jnp.arange(slide_total, dtype=jnp.int32)
    member = (slide_ids[None, :] == slides[:, None]).astype(f32)

    keep_rows = keep_mask.reshape(cells // 128, 128)
    sizes = split_rows(cells)
    starts = [sum(sizes[:c]) for c in range(len(sizes))]
    pieces = [done(first_call(logits, keep_rows, sizes[0]))]
    pipelined = not lead and block % 128 == 0
    one = jnp.where(core == 1, orders[1][0], orders[0][0])
    masks = {"111": 7, "101": 4 + one, "diagonal": 3, "011": 7 - one, "001": 4, "z": 2, "x": 1, "own": 0}
    part_ids = jnp.stack([me ^ mask for mask in masks.values()])
    slot = {name: q for q, name in enumerate(masks)}
    picks = [slot[name] for name in ("111", "101", "diagonal")] if pipelined else []
    outs = exp_call(logits, after(keep_rows), expression, part_ids, picks, sizes)
    pieces += outs[: len(sizes) - 1]
    mapping, sums, *parts = outs[len(sizes) - 1 :]
    done(sums)
    gathered = {}

    def send(c, others=()):
        piece = tie(pieces[c], others)
        for mask in range(2, m, 2):
            gathered[c, mask] = over_spot(piece, mask)

    def spread(c, others=()):
        for mask in range(2, m, 2):
            gathered[c, mask + 1] = over_spot(tie(gathered[c, mask], others), 1)

    def far(c):
        return [gathered[c, mask] for mask in range(2, m, 2)]

    def wide(c):
        return [gathered[c, mask + 1] for mask in range(2, m, 2)]

    send(0)

    part, got, step = {}, {}, {}
    if not picks:
        tops = sum_cell(sums)
        have = dot(expression, mapping, TN).reshape(n, block, spots)
        have = jnp.take(have, ids, axis=0)
        for k in range(lead):
            half = have.shape[0] // 2
            have = have[half:] + across(have[:half].astype(bf16), k).astype(f32)
        for code, q in order.items():
            part[code] = have[q]
        for a in (1, 0):
            for b in (1, 0):
                got[1, a, b] = across(part[1, a, b].astype(bf16), lead)
        for b in (1, 0):
            part[0, 1, b] = add_call([part[0, 1, b], got[1, 1, b]])
            step[0, 1, b] = across(part[0, 1, b], lead + 1)
        part[0, 0, 1] = add_call([part[0, 0, 1], got[1, 0, 1], step[0, 1, 1]])
        last = across(part[0, 0, 1], lead + 2)
        terms = [part[0, 0, 0], got[1, 0, 0], step[0, 1, 0], last]
        send(1)
        send(2)
        spread(0)
    else:
        got["111"], got["101"] = across(parts[0], 0), across(parts[1], 0)
        got["diagonal"] = over_cell(parts[2], 2, 0)

        def products(*some, late=()):
            dtypes = [f32 if name in ("011", "001", "own") else bf16 for name in some]
            picks = [slot[name] for name in some]
            outs = done(part_call(expression, mapping, after(part_ids, late), picks, dtypes))
            part.update(zip(some, outs))

        products("011", "001", "z")
        part["011"], tops = done(
            relay_call([after(part["011"], [*far(0), got["101"], got["diagonal"]]), got["111"]], sums)
        )
        got["011"] = across(part["011"], 1)
        got["z"] = over_cell(part["z"], 2, 0)
        send(1)
        spread(0, [part["011"]])
        products("x", "own", late=wide(0))
        part["001"], tops = done(
            relay_call([after(part["001"]), got["101"], got["011"]], tops)
        )
        last = over_cell(part["001"], 4, 0)
        part["x"] = done(add_call([after(part["x"], [got["z"]]), got["diagonal"]]))
        got["x"] = over_cell(part["x"], 1, 0)
        send(2, [part["x"]])
        terms = [part["own"], got["x"], got["z"], last]
    predicted, predicted_near, gene_sums, tops = done(
        predicted_call(terms, tops, target, after(member))
    )
    _, gene_sums, _, far_sums = sum_spot(gene_sums)
    grad, ends = done(
        grad_call(
            gene_sums, far_sums, predicted_near, target, tops, after(member, far(1))
        )
    )

    have = {(0, 0, 0): grad}
    for k in range(3):
        have[tuple(int(q == k) for q in range(3))] = across(grad, lead + k)
    density = done(density_call(mapping, tops, after(member)))
    _, density, _, far_density = sum_spot(density)
    have[0, 0, 1] = hold_call(
        have[0, 0, 1],
        [far_density, have[1, 0, 0], have[0, 1, 0]],
    )
    have[1, 1, 0] = across(have[0, 1, 0], lead)
    have[0, 1, 1] = across(have[0, 0, 1], lead + 1)
    have[1, 0, 1] = across(have[0, 0, 1], lead)

    slope, weight, more = done(
        diverge_call(
            density,
            far_density,
            keep_mask[None, :],
            slide_counts[None, :],
            mapping,
            tops,
            after(member, [have[0, 0, 1]]),
        )
    )
    ends = ends + more
    ends = ends + across(ends, 0)
    have[0, 1, 1] = hold_call(
        have[0, 1, 1], [*[corner(v) for v in far(2)], have[1, 1, 0], have[1, 0, 1], ends]
    )
    send(3, [have[0, 1, 1]])
    spread(1, [have[0, 1, 1]])
    spread(2, [have[0, 1, 1]])
    have[1, 1, 1] = across(have[0, 1, 1], lead)
    ends = ends + across(ends, 1)
    most = ends
    for k in range(2, levels):
        ends = ends + across(ends, k)
    tail = codes((0,) * lead)
    blocks = [have[c[lead:]] for c in tail]
    if lead:
        blocks = jnp.stack(blocks)
        for k in reversed(range(lead)):
            blocks = jnp.concatenate([across(blocks, k), blocks])
        blocks = [blocks[q] for q in range(n)]

    whole_grad, *shares = regroup_call(blocks, after(ids, [ends, *far(3), *wide(1), *wide(2)]), place[None], m)
    done(shares)
    regrouped = [over_spot(value, mask) if mask else value for mask, value in enumerate(shares)]
    beside = over_spot(tie(mapping, shares), 1)
    spread(3, shares)
    grad_logits, loss = done(
        logit_call(
            expression, whole_grad, mapping, slope, weight, after(ends), tops, slide_total
        )
    )
    near_part = done(
        expr_call(None, mapping, [[beside]], regrouped[:2], after(tops))
    )
    rest = [[gathered[c, mask] for mask in range(2, m)] for c in range(4)]
    grad_expression = expr_call(near_part, None, rest, regrouped[2:], after(tops))
    return (loss.reshape(()), predicted, grad_logits, grad_expression)


def solution(mesh):
    in_specs = (P("cell", "spot"), P("cell", None), P("cell", "spot"), P("cell"), P("spot"), P())
    out_specs = (P(), P("cell", "spot"), P("cell", "spot"), P("cell", "spot"))
    body = functools.partial(per_device, mesh.shape["cell"], mesh.shape["spot"])
    return jax.shard_map(
        body, mesh=mesh, in_specs=in_specs, out_specs=out_specs, check_vma=False
    )
```

```python
import functools

import jax
import jax.numpy as jnp
from jax import lax
from jax.experimental import pallas as pl
from jax.experimental.pallas import tpu as pltpu
from jax.sharding import PartitionSpec as P

density_weight = 32.0
expression_scale = 64.0
norm_eps = 1e-06
f32 = jnp.float32
bf16 = jnp.bfloat16
VMEM_LIMIT = 20 << 20
COST_SHARE = 0.05
NT = (((1,), (1,)), ((), ()))
TN = (((0,), (0,)), ((), ()))


def cost(flops, bytes_accessed, share=COST_SHARE):
    return pl.CostEstimate(
        flops=int(flops * share),
        bytes_accessed=int(bytes_accessed * share),
        transcendentals=0,
    )


ANY = pl.BlockSpec(memory_space=pl.ANY)
HBM = pl.BlockSpec(memory_space=pltpu.HBM)
VMEM = pl.BlockSpec(memory_space=pltpu.VMEM)
SMEM = pl.BlockSpec(memory_space=pltpu.SMEM)


def params():
    return pltpu.CompilerParams(vmem_limit_bytes=VMEM_LIMIT)


def shape(dims, dtype):
    return jax.ShapeDtypeStruct(dims, dtype)


def dot(a, b, dims=(((1,), (0,)), ((), ()))):
    return lax.dot_general(a, b, dims, preferred_element_type=f32)


def halves(value):
    high = value.astype(bf16)
    return high, (value - high.astype(f32)).astype(bf16)


def thirds(value):
    high = value.astype(bf16)
    rest = value - high.astype(f32)
    middle = rest.astype(bf16)
    return high, middle, (rest - middle.astype(f32)).astype(bf16)


def split_rows(cells):
    unit = cells // 64
    return [share * unit for share in (16, 18, 30)]


def column_mask(k_ref, group, spots):
    line = jnp.broadcast_to(k_ref[group : group + 1, :].astype(f32), (128, 128)).T
    return jnp.concatenate([line] * (spots // 128), axis=1)


def in_hbm(value):
    return pltpu.with_memory_space_constraint(value, pltpu.HBM)


def first_call(logits, keep_rows, size):
    spots = logits.shape[1]

    def body(x_ref, k_ref, o_ref, x_buf, k_buf, sem):
        copies = [pltpu.make_async_copy(k_ref, k_buf, sem.at[0])]
        for g in range(size // 128):
            at = pl.ds(g * 128, 128)
            copies.append(pltpu.make_async_copy(x_ref.at[at], x_buf.at[at], sem.at[g + 1]))
        for copy in copies:
            copy.start()
        copies[0].wait()
        for g in range(size // 128):
            at = slice(g * 128, (g + 1) * 128)
            copies[g + 1].wait()
            o_ref[at, :] = (jnp.exp(x_buf[at, :]) * column_mask(k_buf, g, spots)).astype(bf16)

    return pl.pallas_call(
        body,
        in_specs=[HBM, HBM],
        out_specs=VMEM,
        out_shape=shape((size, spots), bf16),
        scratch_shapes=[
            pltpu.VMEM((size, spots), f32),
            pltpu.VMEM(keep_rows.shape, jnp.int32),
            pltpu.SemaphoreType.DMA((size // 128 + 1,)),
        ],
        compiler_params=params(),
        cost_estimate=cost(0, 6 * size * spots),
        name="exp_first",
    )(in_hbm(logits), in_hbm(keep_rows))


def exp_call(logits, keep_rows, expression, ids, picks, sizes):
    cells, spots = logits.shape
    block = expression.shape[1] // ids.shape[0]
    tile = 512
    steps = cells // tile
    slots = min(3, steps)
    starts = [sum(sizes[:c]) for c in range(len(sizes))]
    count = len(picks)

    def body(ids_ref, x_ref, k_ref, e_ref, *refs):
        piece_refs = (None, *refs[: len(sizes) - 1])
        all_ref, s_ref, *refs = refs[len(sizes) - 1 :]
        o_refs, refs = refs[:count], refs[count:]
        u_buf, x_buf, held, acc, k_buf, sem, p_sem, a_sem, e_sem, k_sem = refs
        keep = pltpu.make_async_copy(k_ref, k_buf, k_sem)
        keep.start()

        def fetch(t):
            return pltpu.make_async_copy(
                x_ref.at[pl.ds(t * tile, tile)], x_buf.at[t % slots], sem.at[t % slots]
            )

        for t in range(slots):
            fetch(t).start()
        half = cells // 2

        def hold(h, q):
            at = pl.ds(pl.multiple_of(ids_ref[picks[q]] * block, block), block)
            rows = pl.ds(h * half, half)
            return pltpu.make_async_copy(e_ref.at[rows, at], held.at[q], e_sem.at[q])

        for q in range(count):
            hold(0, q).start()
        total = jnp.zeros((8, spots), f32)
        sent = []
        keep.wait()
        for t in range(steps):
            fetch(t).wait()
            for g in range(tile // 128):
                at = slice(t * tile + g * 128, t * tile + (g + 1) * 128)
                rise = jnp.exp(x_buf[t % slots, g * 128 : (g + 1) * 128, :])
                rise = rise * column_mask(k_buf, t * (tile // 128) + g, spots)
                u_buf[at, :] = rise.astype(bf16)
                total = total + jnp.sum(rise.reshape(16, 8, spots), axis=0)
            if t + slots < steps:
                fetch(t + slots).start()
            for c in range(1, len(sizes)):
                if t * tile < starts[c] + sizes[c] <= (t + 1) * tile:
                    copy = pltpu.make_async_copy(
                        u_buf.at[pl.ds(starts[c], sizes[c])], piece_refs[c], p_sem.at[c]
                    )
                    copy.start()
                    sent.append(copy)
            if t % 2:
                at = pl.ds((t - 1) * tile, 2 * tile)
                copy = pltpu.make_async_copy(u_buf.at[at], all_ref.at[at], a_sem.at[t // 2])
                copy.start()
                sent.append(copy)
            if t == steps // 2 - 1:
                for q in range(count):
                    hold(0, q).wait()
                    acc[q] = dot(held[q], u_buf[0:half, :], TN)
                    hold(1, q).start()
        kept = jnp.full((1, spots), jnp.sum(k_buf[...].astype(f32)), f32)
        total = jnp.sum(total, axis=0, keepdims=True)
        tops = jnp.concatenate([total, kept, jnp.zeros((6, spots), f32)], axis=0)
        s_ref[...] = tops
        for q in range(count):
            hold(1, q).wait()
            term = dot(held[q], u_buf[half:cells, :], TN)
            o_refs[q][0:block, :] = (acc[q] + term).astype(bf16)
            if q == 0:
                o_refs[0][block : block + 16, :] = packed(tops)
        for copy in sent:
            copy.wait()

    return pl.pallas_call(
        body,
        in_specs=[SMEM, HBM, HBM, HBM],
        out_specs=[HBM] * len(sizes) + [VMEM] * (1 + count),
        out_shape=[pltpu.HBM((size, spots), bf16) for size in (*sizes[1:], cells)]
        + [shape((8, spots), f32)]
        + [shape((block + 16 * (q == 0), spots), bf16) for q in range(count)],
        scratch_shapes=[
            pltpu.VMEM((cells, spots), bf16),
            pltpu.VMEM((slots, tile, spots), f32),
            pltpu.VMEM((count, cells // 2, block), bf16),
            pltpu.VMEM((count, block, spots), f32),
            pltpu.VMEM(keep_rows.shape, jnp.int32),
            pltpu.SemaphoreType.DMA((slots,)),
            pltpu.SemaphoreType.DMA((len(sizes),)),
            pltpu.SemaphoreType.DMA((steps // 2,)),
            pltpu.SemaphoreType.DMA((count,)),
            pltpu.SemaphoreType.DMA,
        ],
        compiler_params=params(),
        cost_estimate=cost(0, 8 * cells * spots),
        name="exp_rows",
    )(ids, in_hbm(logits), in_hbm(keep_rows), in_hbm(expression))


def part_call(expression, mapping, ids, picks, dtypes, came):
    cells, spots = mapping.shape
    count = len(picks)
    block = expression.shape[1] // ids.shape[0]

    def body(ids_ref, e_ref, u_ref, *refs):
        came_refs, refs = refs[: len(came)], refs[len(came) :]
        o_refs, (held, sem) = refs[:count], refs[count:]
        copies = []
        for q, pick in enumerate(picks):
            at = pl.ds(pl.multiple_of(ids_ref[pick] * block, block), block)
            copies.append(pltpu.make_async_copy(e_ref.at[:, at], held.at[q], sem.at[q]))
            copies[q].start()
        for q in range(count):
            copies[q].wait()
            total = dot(held[q], u_ref[...], TN)
            for ref in came_refs if q == 0 else ():
                total = total + ref[...].astype(f32)
            o_refs[q][...] = total.astype(dtypes[q])

    return pl.pallas_call(
        body,
        in_specs=[SMEM, HBM, VMEM] + [VMEM] * len(came),
        out_specs=[VMEM] * count,
        out_shape=[shape((block, spots), dtype) for dtype in dtypes],
        scratch_shapes=[
            pltpu.VMEM((count, cells, block), bf16),
            pltpu.SemaphoreType.DMA((count,)),
        ],
        compiler_params=params(),
        cost_estimate=cost(
            2 * count * block * cells * spots, 2 * cells * (count * block + spots)
        ),
        name="part",
    )(ids, in_hbm(expression), mapping, *came)


def add_call(values):
    def body(*refs):
        total = refs[0][...].astype(f32)
        for ref in refs[1:-1]:
            total = total + ref[...].astype(f32)
        refs[-1][...] = total.astype(bf16)

    return pl.pallas_call(
        body,
        out_shape=shape(values[0].shape, bf16),
        compiler_params=params(),
        cost_estimate=cost(0, 8 * values[0].size),
        name="add_blocks",
    )(*values)


def packed(tops):
    rows = jnp.concatenate([part.astype(f32) for part in thirds(tops[0:2, :])], axis=0)
    return jnp.concatenate([rows, jnp.zeros((10, tops.shape[1]), f32)], axis=0).astype(bf16)


def unpacked(rows):
    rows = rows.astype(f32)
    two = rows[0:2, :] + rows[2:4, :] + rows[4:6, :]
    return jnp.concatenate([two, jnp.zeros((6, rows.shape[1]), f32)], axis=0)


def relay_call(values, tops):
    block, spots = values[0].shape

    def body(*refs):
        *v_refs, tops_ref, o_ref, t_ref = refs
        total = v_refs[0][...].astype(f32)
        for ref in v_refs[1:]:
            total = total + ref[0:block, :].astype(f32)
        o_ref[0:block, :] = total.astype(bf16)
        tops_now = tops_ref[...] + unpacked(v_refs[-1][block : block + 16, :])
        t_ref[...] = tops_now
        o_ref[block : block + 16, :] = packed(tops_now)

    return pl.pallas_call(
        body,
        in_specs=[VMEM] * (len(values) + 1),
        out_specs=[VMEM] * 2,
        out_shape=[shape((block + 16, spots), bf16), shape(tops.shape, f32)],
        compiler_params=params(),
        cost_estimate=cost(0, 8 * block * spots),
        name="relay",
    )(*values, tops)


def hold_call(value, others):
    def body(*refs):
        refs[-1][...] = refs[-2][...]

    return pl.pallas_call(
        body,
        in_specs=[VMEM] * (1 + len(others)),
        out_specs=VMEM,
        out_shape=shape(value.shape, value.dtype),
        compiler_params=params(),
        cost_estimate=cost(0, 0),
        name="hold",
    )(*others, value)


def total_of(tops_ref):
    return tops_ref[0:1, :]


def kept_of(tops_ref):
    return tops_ref[1:2, 0:1]


def predicted_call(values, tops, target, member):
    block, spots = target.shape
    slides = member.shape[0]
    more = values[-1].shape[0] > block

    def body(*refs):
        v_refs, (tops_ref, t_ref, m_ref, p_ref, near_ref, s_ref, all_ref) = refs[:-7], refs[-7:]
        total = v_refs[0][...].astype(f32)
        for ref in v_refs[1:]:
            total = total + ref[0:block, :].astype(f32)
        tops_now = tops_ref[...]
        if more:
            tops_now = tops_now + unpacked(v_refs[-1][block : block + 16, :])
        all_ref[...] = tops_now
        pred = total / tops_now[0:1, :]
        p_ref[...] = pred
        near_ref[...] = pred
        target_now = t_ref[...]
        member_low = m_ref[...].astype(bf16)
        for q, value in enumerate((pred * target_now, pred * pred, target_now * target_now)):
            high, low = halves(value)
            s_ref[q * slides : (q + 1) * slides, :] = dot(member_low, high, NT) + dot(
                member_low, low, NT
            )

    return pl.pallas_call(
        body,
        in_specs=[VMEM] * (len(values) + 3),
        out_specs=[VMEM] * 4,
        out_shape=[
            shape((block, spots), f32),
            shape((block, spots), f32),
            shape((3 * slides, block), f32),
            shape(tops.shape, f32),
        ],
        compiler_params=params(),
        cost_estimate=cost(0, 16 * block * spots),
        name="predicted",
    )(*values, tops, target, member)


def grad_call(sums, far, pred, target, tops, member):
    block, spots = target.shape
    slides = member.shape[0]

    def body(s_ref, f_ref, p_ref, t_ref, tops_ref, m_ref, g_ref, e_ref):
        total = s_ref[...] + f_ref[...]
        inner = total[0:slides, :]
        inv_predict = lax.rsqrt(total[slides : 2 * slides, :] + norm_eps)
        inv_target = lax.rsqrt(total[2 * slides : 3 * slides, :] + norm_eps)
        pair = inv_predict * inv_target
        cosine = inner * pair
        member_low = m_ref[...].astype(bf16)
        pair_at = sum(dot(v, member_low, TN) for v in thirds(pair))
        curve_at = sum(dot(v, member_low, TN) for v in thirds(cosine * inv_predict * inv_predict))
        pred = p_ref[...]
        grad = (pred * curve_at - t_ref[...] * pair_at) / total_of(tops_ref)
        grad = grad.astype(bf16)
        g_ref[...] = grad
        column = jnp.sum(pred * grad.astype(f32), axis=0, keepdims=True)
        total = jnp.sum(jnp.sum(cosine, axis=1, keepdims=True), axis=0, keepdims=True)
        e_ref[...] = jnp.concatenate(
            [column, jnp.broadcast_to(total, (1, spots)), jnp.zeros((6, spots), f32)], axis=0
        )

    return pl.pallas_call(
        body,
        out_shape=[shape((block, spots), bf16), shape((8, spots), f32)],
        compiler_params=params(),
        cost_estimate=cost(0, 12 * block * spots),
        name="grad",
    )(sums, far, pred, target, tops, member)


def density_call(mapping, tops, member):
    cells, spots = mapping.shape
    slides = member.shape[0]
    tile = min(cells, 1024)

    def body(u_ref, tops_ref, m_ref, o_ref):
        high, low = halves(m_ref[...] / total_of(tops_ref))
        pad = jnp.zeros((128 - 2 * slides, spots), bf16)
        both = jnp.concatenate([high, low, pad], axis=0)
        for t in range(cells // tile):
            at = slice(t * tile, (t + 1) * tile)
            got = dot(u_ref[at, :], both, NT).T
            o_ref[:, at] = got[0:slides, :] + got[slides : 2 * slides, :]

    return pl.pallas_call(
        body,
        in_specs=[VMEM] * 3,
        out_specs=VMEM,
        out_shape=shape((slides, cells), f32),
        compiler_params=params(),
        cost_estimate=cost(0, 2 * cells * spots),
        name="density",
    )(mapping, tops, member)


def diverge_call(density, far, keep_line, counts, mapping, tops, member):
    cells, spots = mapping.shape
    slides = member.shape[0]

    def body(d_ref, f_ref, k_ref, c_ref, u_ref, tops_ref, m_ref, s_ref, w_ref, e_ref, o_ref, sem):
        keep = k_ref[...].astype(f32)
        kept = kept_of(tops_ref)
        total = total_of(tops_ref)
        safe = jnp.where(keep > 0, d_ref[...] + f_ref[...], 1.0)
        high, low = halves(-density_weight * keep / (kept * safe))
        rest = jnp.concatenate([jnp.ones((8, cells), f32), jnp.zeros((96, cells), f32)], axis=0)
        parts = [high.astype(f32), high.astype(f32), low.astype(f32), rest]
        parts = jnp.concatenate(parts, axis=0)
        w_high, w_low = halves(m_ref[...] / total)
        w_ref[...] = jnp.concatenate([w_high, w_low, w_high, jnp.zeros_like(w_low)], axis=0)
        column = jnp.zeros((8, spots), f32)
        chunk = 256
        for r in range(cells // chunk):
            at = slice(r * chunk, (r + 1) * chunk)
            o_ref[at, :] = parts[:, at].T.astype(bf16)
            pulled = dot(o_ref[at, 0:32], w_ref[...]) * u_ref[at, :].astype(f32)
            column += jnp.sum(pulled.reshape(chunk // 8, 8, spots), axis=0)
        store = pltpu.make_async_copy(o_ref, s_ref, sem)
        store.start()
        column = jnp.sum(column, axis=0, keepdims=True) / total
        logs = jnp.sum(jnp.log(safe), axis=0, keepdims=True)
        logs = -jnp.sum(logs, axis=1, keepdims=True)
        scale = jnp.sum(jnp.log(c_ref[...].astype(f32)), axis=1, keepdims=True)
        scale = scale - slides * jnp.log(kept)
        diverge = (logs + scale * jnp.sum(keep, axis=1, keepdims=True)) / kept
        e_ref[...] = jnp.concatenate(
            [
                column,
                jnp.zeros_like(column),
                jnp.broadcast_to(diverge, (1, spots)),
                jnp.zeros((5, spots), f32),
            ],
            axis=0,
        )
        store.wait()

    return pl.pallas_call(
        body,
        in_specs=[VMEM] * 7,
        out_specs=[HBM, VMEM, VMEM],
        out_shape=[
            pltpu.HBM((cells, 128), bf16),
            shape((4 * slides, spots), bf16),
            shape((8, spots), f32),
        ],
        scratch_shapes=[pltpu.VMEM((cells, 128), bf16), pltpu.SemaphoreType.DMA],
        compiler_params=params(),
        cost_estimate=cost(0, 2 * cells * spots),
        name="diverge",
    )(density, far, keep_line, counts, mapping, tops, member)


def regroup_call(blocks, ids, place, spread):
    count = len(blocks)
    block, spots = blocks[0].shape
    share = count * block // spread

    def body(ids_ref, place_ref, *refs):
        b_refs, all_ref, o_refs = refs[:count], refs[count], refs[count + 1 : count + 1 + spread]
        in_sem, out_sem = refs[count + 1 + spread :]

        def rows(start, size):
            return all_ref.at[pl.ds(pl.multiple_of(start, size), size)]

        copies = [
            pltpu.make_async_copy(b_refs[q], rows(ids_ref[q] * block, block), in_sem.at[q])
            for q in range(count)
        ]
        for copy in copies:
            copy.start()
        for copy in copies:
            copy.wait()
        copies = [
            pltpu.make_async_copy(rows((place_ref[0] ^ w) * share, share), o_refs[w], out_sem.at[w])
            for w in range(spread)
        ]
        for copy in copies:
            copy.start()
        for copy in copies:
            copy.wait()

    return pl.pallas_call(
        body,
        in_specs=[SMEM, SMEM] + [ANY] * count,
        out_specs=[VMEM] + [HBM] * spread,
        out_shape=[shape((count * block, spots), bf16)]
        + [shape((share, spots), bf16)] * spread,
        scratch_shapes=[
            pltpu.SemaphoreType.DMA((count,)),
            pltpu.SemaphoreType.DMA((spread,)),
        ],
        compiler_params=params(),
        cost_estimate=cost(0, 4 * count * block * spots),
        name="regroup",
    )(ids, place, blocks[0], *[in_hbm(value) for value in blocks[1:]])


def logit_call(expression, grad, mapping, slope, weight, ends, tops, slides):
    cells, genes = expression.shape
    spots = grad.shape[1]
    tile = min(cells, 512)
    slots = 3
    runs = [(row, tile) for row in range(0, cells, tile)]

    def body(e_ref, g_ref, u_ref, d_ref, w_ref, ends_ref, tops_ref, *refs):
        o_ref, l_ref, held, e_buf, u_buf, out, in_sem, out_sem = refs

        def fetch(k):
            row, size = runs[k]
            copies = []
            to = (k % slots, pl.ds(0, size))
            copies.append(
                pltpu.make_async_copy(
                    e_ref.at[pl.ds(row, size)], e_buf.at[*to, pl.ds(0, genes)], in_sem.at[k % slots, 0]
                )
            )
            copies.append(
                pltpu.make_async_copy(
                    u_ref.at[pl.ds(row, size)], u_buf.at[*to], in_sem.at[k % slots, 1]
                )
            )
            copies.append(
                pltpu.make_async_copy(
                    d_ref.at[pl.ds(row, size)],
                    e_buf.at[*to, pl.ds(genes, 128)],
                    in_sem.at[k % slots, 2],
                )
            )
            return copies

        def store(k):
            row, size = runs[k]
            return pltpu.make_async_copy(
                out.at[k % 2, pl.ds(0, size)], o_ref.at[pl.ds(row, size)], out_sem.at[k % 2]
            )

        for copy in fetch(0):
            copy.start()
        held[0:genes, :] = g_ref[...]
        sums = jnp.concatenate([part.astype(f32) for part in thirds(-ends_ref[0:1, :])], axis=0)
        sums = jnp.concatenate([sums, jnp.zeros((101, spots), f32)], axis=0)
        weights = jnp.concatenate([w_ref[0:24, :].astype(f32), sums], axis=0)
        held[genes : genes + 128, :] = weights.astype(bf16)
        kept = kept_of(tops_ref)
        total = density_weight * ends_ref[2:3, 0:1] - ends_ref[1:2, 0:1]
        l_ref[...] = total / (genes * slides)
        following = 1
        for k, (row, size) in enumerate(runs):
            for copy in fetch(k):
                copy.wait()
            while following < min(k + slots, len(runs)):
                for copy in fetch(following):
                    copy.start()
                following += 1
            if k >= 2:
                store(k - 2).wait()
            acc = dot(e_buf[k % slots, 0:size], held[...])
            out[k % 2, 0:size] = (u_buf[k % slots, 0:size].astype(f32) * kept) * acc
            store(k).start()
        for k in range(len(runs) - 2, len(runs)):
            store(k).wait()

    return pl.pallas_call(
        body,
        in_specs=[HBM, VMEM, HBM, HBM] + [VMEM] * 3,
        out_specs=[HBM, VMEM],
        out_shape=[pltpu.HBM((cells, spots), f32), shape((1, 1), f32)],
        scratch_shapes=[
            pltpu.VMEM((genes + 128, spots), bf16),
            pltpu.VMEM((slots, tile, genes + 128), bf16),
            pltpu.VMEM((slots, tile, spots), bf16),
            pltpu.VMEM((2, tile, spots), f32),
            pltpu.SemaphoreType.DMA((slots, 3)),
            pltpu.SemaphoreType.DMA((2,)),
        ],
        compiler_params=params(),
        cost_estimate=cost(
            2 * cells * genes * spots, 2 * cells * genes + 6 * cells * spots, 0.0
        ),
        name="grad_logits",
    )(in_hbm(expression), grad, in_hbm(mapping), in_hbm(slope), weight, ends, tops)


def expr_call(base, mapping, beside, chunks, grads, tops):
    genes, spots = grads[0].shape
    cells = mapping.shape[0] if base is None else base.shape[0]
    count = len(grads)
    tile = 512
    own = 0 if mapping is None else 1
    tiles, c, row = [], 0, 0
    for t in range(cells // tile):
        runs, filled = [], 0
        while filled < tile:
            size = min(tile - filled, chunks[c][0].shape[0] - row)
            runs.append((c, row, filled, size))
            filled, row = filled + size, row + size
            if row == chunks[c][0].shape[0]:
                c, row = c + 1, 0
        tiles.append(runs)
    most = max(len(runs) for runs in tiles)
    slots = 3
    flat = [v for chunk in chunks for v in chunk]
    whole = 2 * own
    far = count - whole

    def body(*refs):
        q_refs, refs = refs[: len(flat)], refs[len(flat) :]
        g_refs, refs = refs[:count], refs[count:]
        tops_ref, refs = refs[0], refs[1:]
        w_refs, refs = refs[: whole or 1], refs[whole or 1 :]
        o_ref, held, g_buf, out, in_sem, out_sem = refs
        scale = expression_scale * kept_of(tops_ref)

        def fetch(k):
            pieces = [
                (whole + q, q_refs[c * far + q].at[pl.ds(row, size)], at, size, r)
                for r, (c, row, at, size) in enumerate(tiles[k])
                for q in range(far)
            ]
            for q in range(whole):
                pieces.append((q, w_refs[q].at[pl.ds(k * tile, tile)], 0, tile, 0))
            return [
                pltpu.make_async_copy(
                    source,
                    held.at[k % slots, pl.ds(at, size), pl.ds(q * spots, spots)],
                    in_sem.at[k % slots, q, r],
                )
                for q, source, at, size, r in pieces
            ]

        def store(k):
            return pltpu.make_async_copy(
                out.at[k % 2], o_ref.at[pl.ds(k * tile, tile)], out_sem.at[k % 2]
            )

        for k in range(slots):
            for copy in fetch(k):
                copy.start()
        for q in range(count):
            g_buf[:, q * spots : (q + 1) * spots] = g_refs[q][...]
        for k in range(len(tiles)):
            for copy in fetch(k):
                copy.wait()
            at = slice(k * tile, (k + 1) * tile)
            if own:
                o_ref[at, :] = dot(held[k % slots], g_buf[...], NT) * scale
            else:
                if k >= 2:
                    store(k - 2).wait()
                out[k % 2] = dot(held[k % slots], g_buf[...], NT) * scale + w_refs[0][at, :]
                store(k).start()
            if k + slots < len(tiles):
                for copy in fetch(k + slots):
                    copy.start()
        if not own:
            for k in range(len(tiles) - 2, len(tiles)):
                store(k).wait()

    rows = len(tiles) * tile
    return pl.pallas_call(
        body,
        in_specs=[ANY] * len(flat) + [VMEM] * (count + 1) + ([HBM, ANY] if own else [VMEM]),
        out_specs=VMEM if own else HBM,
        out_shape=shape((cells, genes), f32) if own else pltpu.HBM((cells, genes), f32),
        scratch_shapes=[
            pltpu.VMEM((slots, tile, count * spots), bf16),
            pltpu.VMEM((genes, count * spots), bf16),
            pltpu.VMEM((2, tile, genes), f32),
            pltpu.SemaphoreType.DMA((slots, count, most)),
            pltpu.SemaphoreType.DMA((2,)),
        ],
        compiler_params=params(),
        cost_estimate=cost(
            2 * rows * spots * count * genes, 2 * rows * spots * count + 4 * rows * genes, 0.0
        ),
        name="grad_expression",
    )(*flat, *grads, tops, *([in_hbm(mapping), beside] if own else [base]))


def per_device(n, m, logits, expression, target, keep_mask, slide_ids, slide_counts):
    cells, spots = logits.shape
    genes = expression.shape[1]
    block = genes // n
    slide_total = slide_counts.shape[0]
    levels = n.bit_length() - 1
    lead = levels - 3
    orders = [[1 << k for k in range(levels)] for _ in range(2)]
    orders[1][0], orders[1][1] = 2, 1
    me = lax.axis_index("cell")
    place = lax.axis_index("spot")
    core = place & 1

    def across(value, *levels_of):
        masks = [sum(order[k] for k in levels_of) for order in orders]
        pairs = [(i * m + j, (i ^ masks[j & 1]) * m + j) for i in range(n) for j in range(m)]
        return lax.ppermute(value, ("cell", "spot"), pairs)

    def over_spot(value, mask):
        return lax.ppermute(value, "spot", [(j, j ^ mask) for j in range(m)])

    def over_cell(value, cell_mask, spot_mask):
        pairs = [
            (i * m + j, (i ^ cell_mask) * m + (j ^ spot_mask)) for i in range(n) for j in range(m)
        ]
        return lax.ppermute(value, ("cell", "spot"), pairs)

    def sum_cell(value):
        for k in range(levels):
            value = value + across(value, k)
        return value

    def sum_spot(value):
        first = aside = other = over_spot(value, 1)
        mask = 2
        while mask < m:
            value = value + other
            first = value if mask == 2 else first
            aside = over_cell(value, 1, 0)
            other = over_cell(aside, 1, mask)
            mask *= 2
        return first, value, aside, other

    def tie(value, others):
        return lax.optimization_barrier((value, *others))[0]

    def corner(value):
        return value[:8, :128]

    last_out = []

    def after(value, others=()):
        tied = lax.optimization_barrier((value, *last_out, *others))[0]
        last_out.clear()
        return tied

    def done(outs):
        last_out.append(outs[0] if isinstance(outs, (list, tuple)) else outs)
        return outs

    def place_of(code):
        value = me
        for k in range(levels):
            if code[k]:
                value = value ^ jnp.where(core == 1, orders[1][k], orders[0][k])
        return value

    def codes(prefix):
        out = [prefix]
        while len(out[0]) < levels:
            out = [c + (b,) for c in out for b in (1, 0)]
        return out

    ids = jnp.stack([place_of(c) for c in codes(())])
    order = {c[lead:]: q for q, c in enumerate(codes((0,) * lead))}
    slides = jnp.arange(slide_total, dtype=jnp.int32)
    member = (slide_ids[None, :] == slides[:, None]).astype(f32)

    keep_rows = keep_mask.reshape(cells // 128, 128)
    sizes = split_rows(cells)
    starts = [sum(sizes[:c]) for c in range(len(sizes))]
    pieces = [done(first_call(logits, keep_rows, sizes[0]))]
    pipelined = not lead and block % 128 == 0
    one = jnp.where(core == 1, orders[1][0], orders[0][0])
    masks = {"111": 7, "101": 4 + one, "diagonal": 3, "011": 7 - one, "001": 4, "z": 2, "x": 1, "own": 0}
    part_ids = jnp.stack([me ^ mask for mask in masks.values()])
    slot = {name: q for q, name in enumerate(masks)}
    picks = [slot[name] for name in ("111", "101", "diagonal")] if pipelined else []
    outs = exp_call(logits, after(keep_rows), expression, part_ids, picks, sizes)
    pieces += outs[: len(sizes) - 1]
    mapping, sums, *parts = outs[len(sizes) - 1 :]
    done(sums)
    gathered = {}

    def send(c, others=()):
        piece = tie(pieces[c], others)
        for mask in range(2, m, 2):
            gathered[c, mask] = over_spot(piece, mask)

    def spread(c, others=()):
        for mask in range(2, m, 2):
            gathered[c, mask + 1] = over_spot(tie(gathered[c, mask], others), 1)

    def far(c):
        return [gathered[c, mask] for mask in range(2, m, 2)]

    def wide(c):
        return [gathered[c, mask + 1] for mask in range(2, m, 2)]

    send(0)

    part, got, step = {}, {}, {}
    if not picks:
        tops = sum_cell(sums)
        have = dot(expression, mapping, TN).reshape(n, block, spots)
        have = jnp.take(have, ids, axis=0)
        for k in range(lead):
            half = have.shape[0] // 2
            have = have[half:] + across(have[:half].astype(bf16), k).astype(f32)
        for code, q in order.items():
            part[code] = have[q]
        for a in (1, 0):
            for b in (1, 0):
                got[1, a, b] = across(part[1, a, b].astype(bf16), lead)
        for b in (1, 0):
            part[0, 1, b] = add_call([part[0, 1, b], got[1, 1, b]])
            step[0, 1, b] = across(part[0, 1, b], lead + 1)
        part[0, 0, 1] = add_call([part[0, 0, 1], got[1, 0, 1], step[0, 1, 1]])
        last = across(part[0, 0, 1], lead + 2)
        terms = [part[0, 0, 0], got[1, 0, 0], step[0, 1, 0], last]
        send(1)
        send(2)
        spread(0)
    else:
        got["111"], got["101"] = across(parts[0], 0), across(parts[1], 0)
        got["diagonal"] = over_cell(parts[2], 2, 0)

        def products(*some, late=(), came=()):
            dtypes = [f32 if name in ("011", "001", "own") else bf16 for name in some]
            picks = [slot[name] for name in some]
            outs = done(part_call(expression, mapping, after(part_ids, late), picks, dtypes, came))
            part.update(zip(some, outs))

        products("011", "001", "z")
        part["011"], tops = done(
            relay_call([after(part["011"], [*far(0), got["101"], got["diagonal"]]), got["111"]], sums)
        )
        got["011"] = across(part["011"], 1)
        got["z"] = over_cell(part["z"], 2, 0)
        send(1)
        spread(0, [part["011"]])
        send(2, [part["011"]])
        products("x", "own", late=wide(0), came=[got["diagonal"]])
        part["001"], tops = done(
            relay_call([after(part["001"]), got["101"], got["011"]], tops)
        )
        last = over_cell(part["001"], 4, 0)
        got["x"] = over_cell(part["x"], 1, 0)
        terms = [part["own"], got["x"], got["z"], last]
    predicted, predicted_near, gene_sums, tops = done(
        predicted_call(terms, tops, target, after(member))
    )
    _, gene_sums, _, far_sums = sum_spot(gene_sums)
    grad, ends = done(
        grad_call(
            gene_sums, far_sums, predicted_near, target, tops, after(member, far(1))
        )
    )

    have = {(0, 0, 0): grad, (0, 0, 1): across(grad, lead + 2)}
    density = done(density_call(mapping, tops, after(member)))
    first, density, _, far_density = sum_spot(density)
    near_grad = hold_call(grad, [first])
    have[0, 1, 0], have[1, 0, 0] = across(near_grad, lead + 1), across(near_grad, lead)
    have[0, 0, 1] = hold_call(
        have[0, 0, 1],
        [far_density, have[1, 0, 0], have[0, 1, 0]],
    )
    have[1, 1, 0] = across(have[0, 1, 0], lead)
    have[0, 1, 1] = across(have[0, 0, 1], lead + 1)
    have[1, 0, 1] = across(have[0, 0, 1], lead)

    slope, weight, more = done(
        diverge_call(
            density,
            far_density,
            keep_mask[None, :],
            slide_counts[None, :],
            mapping,
            tops,
            after(member, [have[0, 0, 1]]),
        )
    )
    ends = ends + more
    ends = ends + across(ends, 0)
    have[0, 1, 1] = hold_call(
        have[0, 1, 1], [have[1, 1, 0], have[1, 0, 1], ends]
    )
    spread(1, [have[0, 1, 1]])
    have[1, 1, 1] = across(have[0, 1, 1], lead)
    ends = ends + across(ends, 1)
    most = ends
    for k in range(2, levels):
        ends = ends + across(ends, k)
    tail = codes((0,) * lead)
    blocks = [have[c[lead:]] for c in tail]
    if lead:
        blocks = jnp.stack(blocks)
        for k in reversed(range(lead)):
            blocks = jnp.concatenate([across(blocks, k), blocks])
        blocks = [blocks[q] for q in range(n)]

    whole_grad, *shares = regroup_call(blocks, after(ids, [ends, *far(2), *wide(1)]), place[None], m)
    done(shares)
    regrouped = [over_spot(value, mask) if mask else value for mask, value in enumerate(shares)]
    beside = over_spot(tie(mapping, shares), 1)
    spread(2, shares)
    grad_logits, loss = done(
        logit_call(
            expression, whole_grad, mapping, slope, weight, after(ends), tops, slide_total
        )
    )
    evens = [[gathered[c, mask] for mask in range(2, m, 2)] for c in range(3)]
    some = [regrouped[mask] for mask in (0, 1, *range(2, m, 2))]
    most_of = done(expr_call(None, mapping, beside, evens, some, after(tops)))
    rest = [wide(c) for c in range(3)]
    grad_expression = expr_call(most_of, None, None, rest, regrouped[3::2], after(tops))
    return (loss.reshape(()), predicted, grad_logits, grad_expression)


def solution(mesh):
    in_specs = (P("cell", "spot"), P("cell", None), P("cell", "spot"), P("cell"), P("spot"), P())
    out_specs = (P(), P("cell", "spot"), P("cell", "spot"), P("cell", "spot"))
    body = functools.partial(per_device, mesh.shape["cell"], mesh.shape["spot"])
    return jax.shard_map(
        body, mesh=mesh, in_specs=in_specs, out_specs=out_specs, check_vma=False
    )
```

```python
import functools

import jax
import jax.numpy as jnp
from jax import lax
from jax.experimental import pallas as pl
from jax.experimental.pallas import tpu as pltpu
from jax.sharding import PartitionSpec as P

density_weight = 32.0
expression_scale = 64.0
norm_eps = 1e-06
f32 = jnp.float32
bf16 = jnp.bfloat16
VMEM_LIMIT = 20 << 20
COST_SHARE = 0.05
NT = (((1,), (1,)), ((), ()))
TN = (((0,), (0,)), ((), ()))


def cost(flops, bytes_accessed, share=COST_SHARE):
    return pl.CostEstimate(
        flops=int(flops * share),
        bytes_accessed=int(bytes_accessed * share),
        transcendentals=0,
    )


ANY = pl.BlockSpec(memory_space=pl.ANY)
HBM = pl.BlockSpec(memory_space=pltpu.HBM)
VMEM = pl.BlockSpec(memory_space=pltpu.VMEM)
SMEM = pl.BlockSpec(memory_space=pltpu.SMEM)


def params():
    return pltpu.CompilerParams(vmem_limit_bytes=VMEM_LIMIT)


def shape(dims, dtype):
    return jax.ShapeDtypeStruct(dims, dtype)


def dot(a, b, dims=(((1,), (0,)), ((), ()))):
    return lax.dot_general(a, b, dims, preferred_element_type=f32)


def halves(value):
    high = value.astype(bf16)
    return high, (value - high.astype(f32)).astype(bf16)


def thirds(value):
    high = value.astype(bf16)
    rest = value - high.astype(f32)
    middle = rest.astype(bf16)
    return high, middle, (rest - middle.astype(f32)).astype(bf16)


def split_rows(cells):
    unit = cells // 64
    return [share * unit for share in (16, 18, 30)]


def column_mask(k_ref, group, spots):
    line = jnp.broadcast_to(k_ref[group : group + 1, :].astype(f32), (128, 128)).T
    return jnp.concatenate([line] * (spots // 128), axis=1)


def in_hbm(value):
    return pltpu.with_memory_space_constraint(value, pltpu.HBM)


def first_call(logits, keep_rows, size):
    spots = logits.shape[1]

    def body(x_ref, k_ref, o_ref, x_buf, k_buf, sem):
        copies = [pltpu.make_async_copy(k_ref, k_buf, sem.at[0])]
        for g in range(size // 128):
            at = pl.ds(g * 128, 128)
            copies.append(pltpu.make_async_copy(x_ref.at[at], x_buf.at[at], sem.at[g + 1]))
        for copy in copies:
            copy.start()
        copies[0].wait()
        for g in range(size // 128):
            at = slice(g * 128, (g + 1) * 128)
            copies[g + 1].wait()
            o_ref[at, :] = (jnp.exp(x_buf[at, :]) * column_mask(k_buf, g, spots)).astype(bf16)

    return pl.pallas_call(
        body,
        in_specs=[HBM, HBM],
        out_specs=VMEM,
        out_shape=shape((size, spots), bf16),
        scratch_shapes=[
            pltpu.VMEM((size, spots), f32),
            pltpu.VMEM(keep_rows.shape, jnp.int32),
            pltpu.SemaphoreType.DMA((size // 128 + 1,)),
        ],
        compiler_params=params(),
        cost_estimate=cost(0, 6 * size * spots),
        name="exp_first",
    )(in_hbm(logits), in_hbm(keep_rows))


def exp_call(logits, keep_rows, expression, ids, picks, sizes):
    cells, spots = logits.shape
    block = expression.shape[1] // ids.shape[0]
    tile = 512
    steps = cells // tile
    slots = min(3, steps)
    starts = [sum(sizes[:c]) for c in range(len(sizes))]
    count = len(picks)

    def body(ids_ref, x_ref, k_ref, e_ref, *refs):
        piece_refs = (None, *refs[: len(sizes) - 1])
        all_ref, s_ref, *refs = refs[len(sizes) - 1 :]
        o_refs, refs = refs[:count], refs[count:]
        u_buf, x_buf, held, acc, k_buf, sem, p_sem, a_sem, e_sem, k_sem = refs
        keep = pltpu.make_async_copy(k_ref, k_buf, k_sem)
        keep.start()

        def fetch(t):
            return pltpu.make_async_copy(
                x_ref.at[pl.ds(t * tile, tile)], x_buf.at[t % slots], sem.at[t % slots]
            )

        for t in range(slots):
            fetch(t).start()
        half = cells // 2

        def hold(h, q):
            at = pl.ds(pl.multiple_of(ids_ref[picks[q]] * block, block), block)
            rows = pl.ds(h * half, half)
            return pltpu.make_async_copy(e_ref.at[rows, at], held.at[q], e_sem.at[q])

        for q in range(count):
            hold(0, q).start()
        total = jnp.zeros((8, spots), f32)
        sent = []
        keep.wait()
        for t in range(steps):
            fetch(t).wait()
            for g in range(tile // 128):
                at = slice(t * tile + g * 128, t * tile + (g + 1) * 128)
                rise = jnp.exp(x_buf[t % slots, g * 128 : (g + 1) * 128, :])
                rise = rise * column_mask(k_buf, t * (tile // 128) + g, spots)
                u_buf[at, :] = rise.astype(bf16)
                total = total + jnp.sum(rise.reshape(16, 8, spots), axis=0)
            if t + slots < steps:
                fetch(t + slots).start()
            for c in range(1, len(sizes)):
                if t * tile < starts[c] + sizes[c] <= (t + 1) * tile:
                    copy = pltpu.make_async_copy(
                        u_buf.at[pl.ds(starts[c], sizes[c])], piece_refs[c], p_sem.at[c]
                    )
                    copy.start()
                    sent.append(copy)
            if t % 2:
                at = pl.ds((t - 1) * tile, 2 * tile)
                copy = pltpu.make_async_copy(u_buf.at[at], all_ref.at[at], a_sem.at[t // 2])
                copy.start()
                sent.append(copy)
            if t == steps // 2 - 1:
                for q in range(count):
                    hold(0, q).wait()
                    acc[q] = dot(held[q], u_buf[0:half, :], TN)
                    hold(1, q).start()
        kept = jnp.full((1, spots), jnp.sum(k_buf[...].astype(f32)), f32)
        total = jnp.sum(total, axis=0, keepdims=True)
        tops = jnp.concatenate([total, kept, jnp.zeros((6, spots), f32)], axis=0)
        s_ref[...] = tops
        for q in range(count):
            hold(1, q).wait()
            term = dot(held[q], u_buf[half:cells, :], TN)
            o_refs[q][0:block, :] = (acc[q] + term).astype(bf16)
            if q == 0:
                o_refs[0][block : block + 16, :] = packed(tops)
        for copy in sent:
            copy.wait()

    return pl.pallas_call(
        body,
        in_specs=[SMEM, HBM, HBM, HBM],
        out_specs=[HBM] * len(sizes) + [VMEM] * (1 + count),
        out_shape=[pltpu.HBM((size, spots), bf16) for size in (*sizes[1:], cells)]
        + [shape((8, spots), f32)]
        + [shape((block + 16 * (q == 0), spots), bf16) for q in range(count)],
        scratch_shapes=[
            pltpu.VMEM((cells, spots), bf16),
            pltpu.VMEM((slots, tile, spots), f32),
            pltpu.VMEM((count, cells // 2, block), bf16),
            pltpu.VMEM((count, block, spots), f32),
            pltpu.VMEM(keep_rows.shape, jnp.int32),
            pltpu.SemaphoreType.DMA((slots,)),
            pltpu.SemaphoreType.DMA((len(sizes),)),
            pltpu.SemaphoreType.DMA((steps // 2,)),
            pltpu.SemaphoreType.DMA((count,)),
            pltpu.SemaphoreType.DMA,
        ],
        compiler_params=params(),
        cost_estimate=cost(0, 8 * cells * spots),
        name="exp_rows",
    )(ids, in_hbm(logits), in_hbm(keep_rows), in_hbm(expression))


def part_call(expression, mapping, ids, picks, dtypes, came):
    cells, spots = mapping.shape
    count = len(picks)
    block = expression.shape[1] // ids.shape[0]

    def body(ids_ref, e_ref, u_ref, *refs):
        came_refs, refs = refs[: len(came)], refs[len(came) :]
        o_refs, (held, sem) = refs[:count], refs[count:]
        copies = []
        for q, pick in enumerate(picks):
            at = pl.ds(pl.multiple_of(ids_ref[pick] * block, block), block)
            copies.append(pltpu.make_async_copy(e_ref.at[:, at], held.at[q], sem.at[q]))
            copies[q].start()
        for q in range(count):
            copies[q].wait()
            total = dot(held[q], u_ref[...], TN)
            for ref in came_refs if q == 0 else ():
                total = total + ref[...].astype(f32)
            o_refs[q][...] = total.astype(dtypes[q])

    return pl.pallas_call(
        body,
        in_specs=[SMEM, HBM, VMEM] + [VMEM] * len(came),
        out_specs=[VMEM] * count,
        out_shape=[shape((block, spots), dtype) for dtype in dtypes],
        scratch_shapes=[
            pltpu.VMEM((count, cells, block), bf16),
            pltpu.SemaphoreType.DMA((count,)),
        ],
        compiler_params=params(),
        cost_estimate=cost(
            2 * count * block * cells * spots, 2 * cells * (count * block + spots)
        ),
        name="part",
    )(ids, in_hbm(expression), mapping, *came)


def add_call(values):
    def body(*refs):
        total = refs[0][...].astype(f32)
        for ref in refs[1:-1]:
            total = total + ref[...].astype(f32)
        refs[-1][...] = total.astype(bf16)

    return pl.pallas_call(
        body,
        out_shape=shape(values[0].shape, bf16),
        compiler_params=params(),
        cost_estimate=cost(0, 8 * values[0].size),
        name="add_blocks",
    )(*values)


def packed(tops):
    rows = jnp.concatenate([part.astype(f32) for part in thirds(tops[0:2, :])], axis=0)
    return jnp.concatenate([rows, jnp.zeros((10, tops.shape[1]), f32)], axis=0).astype(bf16)


def unpacked(rows):
    rows = rows.astype(f32)
    two = rows[0:2, :] + rows[2:4, :] + rows[4:6, :]
    return jnp.concatenate([two, jnp.zeros((6, rows.shape[1]), f32)], axis=0)


def relay_call(values, tops):
    block, spots = values[0].shape

    def body(*refs):
        *v_refs, tops_ref, o_ref, t_ref = refs
        total = v_refs[0][...].astype(f32)
        for ref in v_refs[1:]:
            total = total + ref[0:block, :].astype(f32)
        o_ref[0:block, :] = total.astype(bf16)
        tops_now = tops_ref[...] + unpacked(v_refs[-1][block : block + 16, :])
        t_ref[...] = tops_now
        o_ref[block : block + 16, :] = packed(tops_now)

    return pl.pallas_call(
        body,
        in_specs=[VMEM] * (len(values) + 1),
        out_specs=[VMEM] * 2,
        out_shape=[shape((block + 16, spots), bf16), shape(tops.shape, f32)],
        compiler_params=params(),
        cost_estimate=cost(0, 8 * block * spots),
        name="relay",
    )(*values, tops)


def hold_call(value, others):
    def body(*refs):
        refs[-1][...] = refs[-2][...]

    return pl.pallas_call(
        body,
        in_specs=[VMEM] * (1 + len(others)),
        out_specs=VMEM,
        out_shape=shape(value.shape, value.dtype),
        compiler_params=params(),
        cost_estimate=cost(0, 0),
        name="hold",
    )(*others, value)


def total_of(tops_ref):
    return tops_ref[0:1, :]


def kept_of(tops_ref):
    return tops_ref[1:2, 0:1]


def predicted_call(values, tops, target, member):
    block, spots = target.shape
    slides = member.shape[0]
    more = values[-1].shape[0] > block

    def body(*refs):
        v_refs, (tops_ref, t_ref, m_ref, p_ref, near_ref, s_ref, all_ref) = refs[:-7], refs[-7:]
        total = v_refs[0][...].astype(f32)
        for ref in v_refs[1:]:
            total = total + ref[0:block, :].astype(f32)
        tops_now = tops_ref[...]
        if more:
            tops_now = tops_now + unpacked(v_refs[-1][block : block + 16, :])
        all_ref[...] = tops_now
        pred = total / tops_now[0:1, :]
        p_ref[...] = pred
        near_ref[...] = pred
        target_now = t_ref[...]
        member_low = m_ref[...].astype(bf16)
        for q, value in enumerate((pred * target_now, pred * pred, target_now * target_now)):
            high, low = halves(value)
            s_ref[q * slides : (q + 1) * slides, :] = dot(member_low, high, NT) + dot(
                member_low, low, NT
            )

    return pl.pallas_call(
        body,
        in_specs=[VMEM] * (len(values) + 3),
        out_specs=[VMEM] * 4,
        out_shape=[
            shape((block, spots), f32),
            shape((block, spots), f32),
            shape((3 * slides, block), f32),
            shape(tops.shape, f32),
        ],
        compiler_params=params(),
        cost_estimate=cost(0, 16 * block * spots),
        name="predicted",
    )(*values, tops, target, member)


def grad_call(sums, far, pred, target, tops, member):
    block, spots = target.shape
    slides = member.shape[0]

    def body(s_ref, f_ref, p_ref, t_ref, tops_ref, m_ref, g_ref, e_ref):
        total = s_ref[...] + f_ref[...]
        inner = total[0:slides, :]
        inv_predict = lax.rsqrt(total[slides : 2 * slides, :] + norm_eps)
        inv_target = lax.rsqrt(total[2 * slides : 3 * slides, :] + norm_eps)
        pair = inv_predict * inv_target
        cosine = inner * pair
        member_low = m_ref[...].astype(bf16)
        pair_at = sum(dot(v, member_low, TN) for v in thirds(pair))
        curve_at = sum(dot(v, member_low, TN) for v in thirds(cosine * inv_predict * inv_predict))
        pred = p_ref[...]
        grad = (pred * curve_at - t_ref[...] * pair_at) / total_of(tops_ref)
        grad = grad.astype(bf16)
        g_ref[...] = grad
        column = jnp.sum(pred * grad.astype(f32), axis=0, keepdims=True)
        total = jnp.sum(jnp.sum(cosine, axis=1, keepdims=True), axis=0, keepdims=True)
        e_ref[...] = jnp.concatenate(
            [column, jnp.broadcast_to(total, (1, spots)), jnp.zeros((6, spots), f32)], axis=0
        )

    return pl.pallas_call(
        body,
        out_shape=[shape((block, spots), bf16), shape((8, spots), f32)],
        compiler_params=params(),
        cost_estimate=cost(0, 12 * block * spots),
        name="grad",
    )(sums, far, pred, target, tops, member)


def density_call(mapping, tops, member):
    cells, spots = mapping.shape
    slides = member.shape[0]
    tile = min(cells, 1024)

    def body(u_ref, tops_ref, m_ref, o_ref):
        high, low = halves(m_ref[...] / total_of(tops_ref))
        pad = jnp.zeros((128 - 2 * slides, spots), bf16)
        both = jnp.concatenate([high, low, pad], axis=0)
        for t in range(cells // tile):
            at = slice(t * tile, (t + 1) * tile)
            got = dot(u_ref[at, :], both, NT).T
            o_ref[:, at] = got[0:slides, :] + got[slides : 2 * slides, :]

    return pl.pallas_call(
        body,
        in_specs=[VMEM] * 3,
        out_specs=VMEM,
        out_shape=shape((slides, cells), f32),
        compiler_params=params(),
        cost_estimate=cost(0, 2 * cells * spots),
        name="density",
    )(mapping, tops, member)


def diverge_call(density, far, keep_line, counts, mapping, tops, member):
    cells, spots = mapping.shape
    slides = member.shape[0]

    def body(d_ref, f_ref, k_ref, c_ref, u_ref, tops_ref, m_ref, s_ref, w_ref, e_ref, o_ref, sem):
        keep = k_ref[...].astype(f32)
        kept = kept_of(tops_ref)
        total = total_of(tops_ref)
        safe = jnp.where(keep > 0, d_ref[...] + f_ref[...], 1.0)
        high, low = halves(-density_weight * keep / (kept * safe))
        rest = jnp.concatenate([jnp.ones((8, cells), f32), jnp.zeros((96, cells), f32)], axis=0)
        parts = [high.astype(f32), high.astype(f32), low.astype(f32), rest]
        parts = jnp.concatenate(parts, axis=0)
        w_high, w_low = halves(m_ref[...] / total)
        w_ref[...] = jnp.concatenate([w_high, w_low, w_high, jnp.zeros_like(w_low)], axis=0)
        column = jnp.zeros((8, spots), f32)
        chunk = 256
        for r in range(cells // chunk):
            at = slice(r * chunk, (r + 1) * chunk)
            o_ref[at, :] = parts[:, at].T.astype(bf16)
            pulled = dot(o_ref[at, 0:32], w_ref[...]) * u_ref[at, :].astype(f32)
            column += jnp.sum(pulled.reshape(chunk // 8, 8, spots), axis=0)
        store = pltpu.make_async_copy(o_ref, s_ref, sem)
        store.start()
        column = jnp.sum(column, axis=0, keepdims=True) / total
        logs = jnp.sum(jnp.log(safe), axis=0, keepdims=True)
        logs = -jnp.sum(logs, axis=1, keepdims=True)
        scale = jnp.sum(jnp.log(c_ref[...].astype(f32)), axis=1, keepdims=True)
        scale = scale - slides * jnp.log(kept)
        diverge = (logs + scale * jnp.sum(keep, axis=1, keepdims=True)) / kept
        e_ref[...] = jnp.concatenate(
            [
                column,
                jnp.zeros_like(column),
                jnp.broadcast_to(diverge, (1, spots)),
                jnp.zeros((5, spots), f32),
            ],
            axis=0,
        )
        store.wait()

    return pl.pallas_call(
        body,
        in_specs=[VMEM] * 7,
        out_specs=[HBM, VMEM, VMEM],
        out_shape=[
            pltpu.HBM((cells, 128), bf16),
            shape((4 * slides, spots), bf16),
            shape((8, spots), f32),
        ],
        scratch_shapes=[pltpu.VMEM((cells, 128), bf16), pltpu.SemaphoreType.DMA],
        compiler_params=params(),
        cost_estimate=cost(0, 2 * cells * spots),
        name="diverge",
    )(density, far, keep_line, counts, mapping, tops, member)


def regroup_call(blocks, ids, place, spread):
    count = len(blocks)
    block, spots = blocks[0].shape
    share = count * block // spread

    def body(ids_ref, place_ref, *refs):
        b_refs, all_ref, o_refs = refs[:count], refs[count], refs[count + 1 : count + 1 + spread]
        in_sem, out_sem = refs[count + 1 + spread :]

        def rows(start, size):
            return all_ref.at[pl.ds(pl.multiple_of(start, size), size)]

        copies = [
            pltpu.make_async_copy(b_refs[q], rows(ids_ref[q] * block, block), in_sem.at[q])
            for q in range(count)
        ]
        for copy in copies:
            copy.start()
        for copy in copies:
            copy.wait()
        copies = [
            pltpu.make_async_copy(rows((place_ref[0] ^ w) * share, share), o_refs[w], out_sem.at[w])
            for w in range(spread)
        ]
        for copy in copies:
            copy.start()
        for copy in copies:
            copy.wait()

    return pl.pallas_call(
        body,
        in_specs=[SMEM, SMEM] + [ANY] * count,
        out_specs=[VMEM] + [HBM] * spread,
        out_shape=[shape((count * block, spots), bf16)]
        + [shape((share, spots), bf16)] * spread,
        scratch_shapes=[
            pltpu.SemaphoreType.DMA((count,)),
            pltpu.SemaphoreType.DMA((spread,)),
        ],
        compiler_params=params(),
        cost_estimate=cost(0, 4 * count * block * spots),
        name="regroup",
    )(ids, place, blocks[0], *[in_hbm(value) for value in blocks[1:]])


def logit_call(expression, grad, mapping, slope, weight, ends, tops, slides):
    cells, genes = expression.shape
    spots = grad.shape[1]
    tile = min(cells, 512)
    slots = 3
    runs = [(row, tile) for row in range(0, cells, tile)]

    def body(e_ref, g_ref, u_ref, d_ref, w_ref, ends_ref, tops_ref, *refs):
        o_ref, l_ref, held, e_buf, u_buf, out, in_sem, out_sem = refs

        def fetch(k):
            row, size = runs[k]
            copies = []
            to = (k % slots, pl.ds(0, size))
            copies.append(
                pltpu.make_async_copy(
                    e_ref.at[pl.ds(row, size)], e_buf.at[*to, pl.ds(0, genes)], in_sem.at[k % slots, 0]
                )
            )
            copies.append(
                pltpu.make_async_copy(
                    u_ref.at[pl.ds(row, size)], u_buf.at[*to], in_sem.at[k % slots, 1]
                )
            )
            copies.append(
                pltpu.make_async_copy(
                    d_ref.at[pl.ds(row, size)],
                    e_buf.at[*to, pl.ds(genes, 128)],
                    in_sem.at[k % slots, 2],
                )
            )
            return copies

        def store(k):
            row, size = runs[k]
            return pltpu.make_async_copy(
                out.at[k % 3, pl.ds(0, size)], o_ref.at[pl.ds(row, size)], out_sem.at[k % 3]
            )

        for copy in fetch(0):
            copy.start()
        held[0:genes, :] = g_ref[...]
        sums = jnp.concatenate([part.astype(f32) for part in thirds(-ends_ref[0:1, :])], axis=0)
        sums = jnp.concatenate([sums, jnp.zeros((101, spots), f32)], axis=0)
        weights = jnp.concatenate([w_ref[0:24, :].astype(f32), sums], axis=0)
        held[genes : genes + 128, :] = weights.astype(bf16)
        kept = kept_of(tops_ref)
        total = density_weight * ends_ref[2:3, 0:1] - ends_ref[1:2, 0:1]
        l_ref[...] = total / (genes * slides)
        following = 1
        for k, (row, size) in enumerate(runs):
            for copy in fetch(k):
                copy.wait()
            while following < min(k + slots, len(runs)):
                for copy in fetch(following):
                    copy.start()
                following += 1
            if k >= 3:
                store(k - 3).wait()
            acc = dot(e_buf[k % slots, 0:size], held[...])
            out[k % 3, 0:size] = (u_buf[k % slots, 0:size].astype(f32) * kept) * acc
            store(k).start()
        for k in range(len(runs) - 3, len(runs)):
            store(k).wait()

    return pl.pallas_call(
        body,
        in_specs=[HBM, VMEM, HBM, HBM] + [VMEM] * 3,
        out_specs=[HBM, VMEM],
        out_shape=[pltpu.HBM((cells, spots), f32), shape((1, 1), f32)],
        scratch_shapes=[
            pltpu.VMEM((genes + 128, spots), bf16),
            pltpu.VMEM((slots, tile, genes + 128), bf16),
            pltpu.VMEM((slots, tile, spots), bf16),
            pltpu.VMEM((3, tile, spots), f32),
            pltpu.SemaphoreType.DMA((slots, 3)),
            pltpu.SemaphoreType.DMA((3,)),
        ],
        compiler_params=params(),
        cost_estimate=cost(
            2 * cells * genes * spots, 2 * cells * genes + 6 * cells * spots, 0.0
        ),
        name="grad_logits",
    )(in_hbm(expression), grad, in_hbm(mapping), in_hbm(slope), weight, ends, tops)


def expr_call(base, mapping, beside, chunks, grads, tops):
    genes, spots = grads[0].shape
    cells = mapping.shape[0] if base is None else base.shape[0]
    count = len(grads)
    tile = 512
    own = 0 if mapping is None else 1
    tiles, c, row = [], 0, 0
    for t in range(cells // tile):
        runs, filled = [], 0
        while filled < tile:
            size = min(tile - filled, chunks[c][0].shape[0] - row)
            runs.append((c, row, filled, size))
            filled, row = filled + size, row + size
            if row == chunks[c][0].shape[0]:
                c, row = c + 1, 0
        tiles.append(runs)
    most = max(len(runs) for runs in tiles)
    slots = 3
    flat = [v for chunk in chunks for v in chunk]
    whole = 2 * own
    far = count - whole

    def body(*refs):
        q_refs, refs = refs[: len(flat)], refs[len(flat) :]
        g_refs, refs = refs[:count], refs[count:]
        tops_ref, refs = refs[0], refs[1:]
        w_refs, refs = refs[: whole or 1], refs[whole or 1 :]
        o_ref, held, g_buf, out, in_sem, out_sem = refs
        scale = expression_scale * kept_of(tops_ref)

        def fetch(k):
            pieces = [
                (whole + q, q_refs[c * far + q].at[pl.ds(row, size)], at, size, r)
                for r, (c, row, at, size) in enumerate(tiles[k])
                for q in range(far)
            ]
            for q in range(whole):
                pieces.append((q, w_refs[q].at[pl.ds(k * tile, tile)], 0, tile, 0))
            return [
                pltpu.make_async_copy(
                    source,
                    held.at[k % slots, pl.ds(at, size), pl.ds(q * spots, spots)],
                    in_sem.at[k % slots, q, r],
                )
                for q, source, at, size, r in pieces
            ]

        def store(k):
            return pltpu.make_async_copy(
                out.at[k % 3], o_ref.at[pl.ds(k * tile, tile)], out_sem.at[k % 3]
            )

        for k in range(slots):
            for copy in fetch(k):
                copy.start()
        for q in range(count):
            g_buf[:, q * spots : (q + 1) * spots] = g_refs[q][...]
        for k in range(len(tiles)):
            for copy in fetch(k):
                copy.wait()
            at = slice(k * tile, (k + 1) * tile)
            if own:
                o_ref[at, :] = dot(held[k % slots], g_buf[...], NT) * scale
            else:
                if k >= 3:
                    store(k - 3).wait()
                out[k % 3] = dot(held[k % slots], g_buf[...], NT) * scale + w_refs[0][at, :]
                store(k).start()
            if k + slots < len(tiles):
                for copy in fetch(k + slots):
                    copy.start()
        if not own:
            for k in range(len(tiles) - 3, len(tiles)):
                store(k).wait()

    rows = len(tiles) * tile
    return pl.pallas_call(
        body,
        in_specs=[ANY] * len(flat) + [VMEM] * (count + 1) + ([HBM, ANY] if own else [VMEM]),
        out_specs=VMEM if own else HBM,
        out_shape=shape((cells, genes), f32) if own else pltpu.HBM((cells, genes), f32),
        scratch_shapes=[
            pltpu.VMEM((slots, tile, count * spots), bf16),
            pltpu.VMEM((genes, count * spots), bf16),
            pltpu.VMEM((3, tile, genes), f32),
            pltpu.SemaphoreType.DMA((slots, count, most)),
            pltpu.SemaphoreType.DMA((3,)),
        ],
        compiler_params=params(),
        cost_estimate=cost(
            2 * rows * spots * count * genes, 2 * rows * spots * count + 4 * rows * genes, 0.0
        ),
        name="grad_expression",
    )(*flat, *grads, tops, *([in_hbm(mapping), beside] if own else [base]))


def per_device(n, m, logits, expression, target, keep_mask, slide_ids, slide_counts):
    cells, spots = logits.shape
    genes = expression.shape[1]
    block = genes // n
    slide_total = slide_counts.shape[0]
    levels = n.bit_length() - 1
    lead = levels - 3
    orders = [[1 << k for k in range(levels)] for _ in range(2)]
    orders[1][0], orders[1][1] = 2, 1
    me = lax.axis_index("cell")
    place = lax.axis_index("spot")
    core = place & 1

    def across(value, *levels_of):
        masks = [sum(order[k] for k in levels_of) for order in orders]
        pairs = [(i * m + j, (i ^ masks[j & 1]) * m + j) for i in range(n) for j in range(m)]
        return lax.ppermute(value, ("cell", "spot"), pairs)

    def over_spot(value, mask):
        return lax.ppermute(value, "spot", [(j, j ^ mask) for j in range(m)])

    def over_cell(value, cell_mask, spot_mask):
        pairs = [
            (i * m + j, (i ^ cell_mask) * m + (j ^ spot_mask)) for i in range(n) for j in range(m)
        ]
        return lax.ppermute(value, ("cell", "spot"), pairs)

    def sum_cell(value):
        for k in range(levels):
            value = value + across(value, k)
        return value

    def sum_spot(value):
        first = aside = other = over_spot(value, 1)
        mask = 2
        while mask < m:
            value = value + other
            first = value if mask == 2 else first
            aside = over_cell(value, 1, 0)
            other = over_cell(aside, 1, mask)
            mask *= 2
        return first, value, aside, other

    def tie(value, others):
        return lax.optimization_barrier((value, *others))[0]

    def corner(value):
        return value[:8, :128]

    last_out = []

    def after(value, others=()):
        tied = lax.optimization_barrier((value, *last_out, *others))[0]
        last_out.clear()
        return tied

    def done(outs):
        last_out.append(outs[0] if isinstance(outs, (list, tuple)) else outs)
        return outs

    def place_of(code):
        value = me
        for k in range(levels):
            if code[k]:
                value = value ^ jnp.where(core == 1, orders[1][k], orders[0][k])
        return value

    def codes(prefix):
        out = [prefix]
        while len(out[0]) < levels:
            out = [c + (b,) for c in out for b in (1, 0)]
        return out

    ids = jnp.stack([place_of(c) for c in codes(())])
    order = {c[lead:]: q for q, c in enumerate(codes((0,) * lead))}
    slides = jnp.arange(slide_total, dtype=jnp.int32)
    member = (slide_ids[None, :] == slides[:, None]).astype(f32)

    keep_rows = keep_mask.reshape(cells // 128, 128)
    sizes = split_rows(cells)
    starts = [sum(sizes[:c]) for c in range(len(sizes))]
    pieces = [done(first_call(logits, keep_rows, sizes[0]))]
    pipelined = not lead and block % 128 == 0
    one = jnp.where(core == 1, orders[1][0], orders[0][0])
    masks = {"111": 7, "101": 4 + one, "diagonal": 3, "011": 7 - one, "001": 4, "z": 2, "x": 1, "own": 0}
    part_ids = jnp.stack([me ^ mask for mask in masks.values()])
    slot = {name: q for q, name in enumerate(masks)}
    picks = [slot[name] for name in ("111", "101", "diagonal")] if pipelined else []
    outs = exp_call(logits, after(keep_rows), expression, part_ids, picks, sizes)
    pieces += outs[: len(sizes) - 1]
    mapping, sums, *parts = outs[len(sizes) - 1 :]
    done(sums)
    gathered = {}

    def send(c, others=()):
        piece = tie(pieces[c], others)
        for mask in range(2, m, 2):
            gathered[c, mask] = over_spot(piece, mask)

    def spread(c, others=()):
        for mask in range(2, m, 2):
            gathered[c, mask + 1] = over_spot(tie(gathered[c, mask], others), 1)

    def far(c):
        return [gathered[c, mask] for mask in range(2, m, 2)]

    def wide(c):
        return [gathered[c, mask + 1] for mask in range(2, m, 2)]

    send(0)

    part, got, step = {}, {}, {}
    if not picks:
        tops = sum_cell(sums)
        have = dot(expression, mapping, TN).reshape(n, block, spots)
        have = jnp.take(have, ids, axis=0)
        for k in range(lead):
            half = have.shape[0] // 2
            have = have[half:] + across(have[:half].astype(bf16), k).astype(f32)
        for code, q in order.items():
            part[code] = have[q]
        for a in (1, 0):
            for b in (1, 0):
                got[1, a, b] = across(part[1, a, b].astype(bf16), lead)
        for b in (1, 0):
            part[0, 1, b] = add_call([part[0, 1, b], got[1, 1, b]])
            step[0, 1, b] = across(part[0, 1, b], lead + 1)
        part[0, 0, 1] = add_call([part[0, 0, 1], got[1, 0, 1], step[0, 1, 1]])
        last = across(part[0, 0, 1], lead + 2)
        terms = [part[0, 0, 0], got[1, 0, 0], step[0, 1, 0], last]
        send(1)
        send(2)
        spread(0)
    else:
        got["111"], got["101"] = across(parts[0], 0), across(parts[1], 0)
        got["diagonal"] = over_cell(parts[2], 2, 0)

        def products(*some, late=(), came=()):
            dtypes = [f32 if name in ("011", "001", "own") else bf16 for name in some]
            picks = [slot[name] for name in some]
            outs = done(part_call(expression, mapping, after(part_ids, late), picks, dtypes, came))
            part.update(zip(some, outs))

        products("011", "001", "z")
        part["011"], tops = done(
            relay_call([after(part["011"], [*far(0), got["101"], got["diagonal"]]), got["111"]], sums)
        )
        got["011"] = across(part["011"], 1)
        got["z"] = over_cell(part["z"], 2, 0)
        send(1)
        spread(0, [part["011"]])
        send(2, [part["011"]])
        products("x", "own", late=wide(0), came=[got["diagonal"]])
        part["001"], tops = done(
            relay_call([after(part["001"]), got["101"], got["011"]], tops)
        )
        last = over_cell(part["001"], 4, 0)
        got["x"] = over_cell(part["x"], 1, 0)
        terms = [part["own"], got["x"], got["z"], last]
    predicted, predicted_near, gene_sums, tops = done(
        predicted_call(terms, tops, target, after(member))
    )
    _, gene_sums, _, far_sums = sum_spot(gene_sums)
    grad, ends = done(
        grad_call(
            gene_sums, far_sums, predicted_near, target, tops, after(member, far(1))
        )
    )

    have = {(0, 0, 0): grad, (0, 0, 1): across(grad, lead + 2)}
    density = done(density_call(mapping, tops, after(member)))
    first, density, _, far_density = sum_spot(density)
    near_grad = hold_call(grad, [first])
    have[0, 1, 0], have[1, 0, 0] = across(near_grad, lead + 1), across(near_grad, lead)
    have[0, 0, 1] = hold_call(
        have[0, 0, 1],
        [far_density, have[1, 0, 0], have[0, 1, 0]],
    )
    have[1, 1, 0] = across(have[0, 1, 0], lead)
    have[0, 1, 1] = across(have[0, 0, 1], lead + 1)
    have[1, 0, 1] = across(have[0, 0, 1], lead)

    slope, weight, more = done(
        diverge_call(
            density,
            far_density,
            keep_mask[None, :],
            slide_counts[None, :],
            mapping,
            tops,
            after(member, [have[0, 0, 1]]),
        )
    )
    ends = ends + more
    ends = ends + across(ends, 0)
    have[0, 1, 1] = hold_call(
        have[0, 1, 1], [have[1, 1, 0], have[1, 0, 1], ends]
    )
    spread(1, [have[0, 1, 1]])
    have[1, 1, 1] = across(have[0, 1, 1], lead)
    ends = ends + across(ends, 1)
    most = ends
    for k in range(2, levels):
        ends = ends + across(ends, k)
    tail = codes((0,) * lead)
    blocks = [have[c[lead:]] for c in tail]
    if lead:
        blocks = jnp.stack(blocks)
        for k in reversed(range(lead)):
            blocks = jnp.concatenate([across(blocks, k), blocks])
        blocks = [blocks[q] for q in range(n)]

    whole_grad, *shares = regroup_call(blocks, after(ids, [ends, *far(2), *wide(1)]), place[None], m)
    done(shares)
    regrouped = [over_spot(value, mask) if mask else value for mask, value in enumerate(shares)]
    beside = over_spot(tie(mapping, shares), 1)
    spread(2, shares)
    grad_logits, loss = done(
        logit_call(
            expression, whole_grad, mapping, slope, weight, after(ends), tops, slide_total
        )
    )
    evens = [[gathered[c, mask] for mask in range(2, m, 2)] for c in range(3)]
    some = [regrouped[mask] for mask in (0, 1, *range(2, m, 2))]
    most_of = done(expr_call(None, mapping, beside, evens, some, after(tops)))
    rest = [wide(c) for c in range(3)]
    grad_expression = expr_call(most_of, None, None, rest, regrouped[3::2], after(tops))
    return (loss.reshape(()), predicted, grad_logits, grad_expression)


def solution(mesh):
    in_specs = (P("cell", "spot"), P("cell", None), P("cell", "spot"), P("cell"), P("spot"), P())
    out_specs = (P(), P("cell", "spot"), P("cell", "spot"), P("cell", "spot"))
    body = functools.partial(per_device, mesh.shape["cell"], mesh.shape["spot"])
    return jax.shard_map(
        body, mesh=mesh, in_specs=in_specs, out_specs=out_specs, check_vma=False
    )
```
